128 devices in a mesh: dp: 8 (over x, core), tensor: 16 (over z, y).
Axes of the slice: x: 4, y: 4, z: 4, core: 2. Of those that a mesh axis runs over, the one named last changes fastest.
Arguments:
- hidden: bfloat16 [2, 2048, 5120], P(None, 'dp', 'tensor'), may hold values from -48 to 48
- draft_head: bfloat16 [5120, 24000], P(None, 'tensor'), may hold values from -0.09782797 to 0.09782797
- target_logits: bfloat16 [2048, 151936], P('dp', 'tensor'), may hold values from -320 to 320
- draft_to_target: int32 [24000], replicated, may hold values from 0 to 151935, as said below
Outputs:
- grad_hidden: bfloat16 [2, 2048, 5120], P(None, 'dp', 'tensor')
- grad_head: float32 [5120, 24000], P('dp', 'tensor')
The draws below stay inside these ranges and needn't reach their ends.
Inputs may be any that keep to these rules, and one draw needn't show every extreme that they name: `draft_to_target`: all ids are distinct. Of the 1500 draft ids of one aligned block, at most 270 lie in any one aligned block of 9496 target ids, and in every draft block exactly 270 lie in one target block.
All inputs are finite; a program needn't handle non-finite values.
Results may differ from the reference program's by a relative error of at most 0.0054.
Values may be sent and summed in bfloat16 or wider, within the bound.
A program may use at most 192 MiB of HBM per device.

```python
import math
import jax
import jax.numpy as jnp

D = 5120
VT = 151936
VD = 24000
TOK_DEV = 256
STEPS = 2
TOKENS = 2048
N_DP = 8
N_TENSOR = 16


def head_base(key):
    return jnp.clip(jax.random.normal(key, (D, VD), jnp.float32), -6.0, 6.0) / math.sqrt(D)


def draw_draft_head(key, part):
    return head_base(key).astype(jnp.bfloat16)


def draw_hidden(key, part):
    key = jax.random.fold_in(key, 11)
    first = jax.random.fold_in(key, 0)
    result = jnp.clip(jax.random.normal(first, (STEPS, TOKENS, D), jnp.float32), -5.0, 5.0)
    return result.astype(jnp.bfloat16)


def draw_target_logits(key, part):
    key = jax.random.fold_in(key, 23)
    first = jax.random.fold_in(key, 0)
    result = jnp.clip(3.0 * jax.random.normal(first, (TOKENS, VT), jnp.float32), -15.0, 15.0)
    return result.astype(jnp.bfloat16)


def draw_draft_to_target(key, part):
    key = jax.random.fold_in(key, 37)
    first, second, third = jax.random.split(key, 3)
    block = VD // N_TENSOR
    shelf = VT // N_TENSOR
    heavy = block // 8
    bound = heavy + (block - heavy + N_TENSOR - 1) // N_TENSOR
    ranks = jax.vmap(lambda k: jax.random.permutation(k, block))(jax.random.split(first, N_TENSOR))
    chosen = jax.random.randint(second, (N_TENSOR, 1), 0, N_TENSOR)
    rest = ranks - heavy
    owner = jnp.where(ranks < heavy, chosen, (rest + chosen) % N_TENSOR)
    slot = jnp.where(ranks < heavy, ranks, rest // N_TENSOR + jnp.where(owner == chosen, heavy, 0))
    shelves = jax.vmap(lambda k: jax.random.permutation(k, shelf))(jax.random.split(third, N_TENSOR))
    position = jnp.arange(N_TENSOR)[:, None] * bound + slot
    local = shelves[owner, position]
    return (owner * shelf + local).reshape(VD).astype(jnp.int32)


def setup_inputs(seed: int = 0) -> dict:
    key_list = jax.random.split(jax.random.key(seed), 5)
    hidden = draw_hidden(jax.random.fold_in(key_list[4], 71), 0)
    draft_head = draw_draft_head(jax.random.fold_in(key_list[4], 71), 0)
    target_logits = draw_target_logits(jax.random.fold_in(key_list[4], 71), 0)
    draft_to_target = draw_draft_to_target(jax.random.fold_in(key_list[4], 71), 0)
    return dict(hidden=hidden, draft_head=draft_head, target_logits=target_logits, draft_to_target=draft_to_target)


LOSS_SCALE = 256.0
STEP_DECAY = 0.8


def reference(hidden, draft_head, target_logits, draft_to_target):
    logits = target_logits.astype(jnp.float32)
    peak = jnp.max(logits, axis=1, keepdims=True)
    total = jnp.sum(jnp.exp(logits - peak), axis=1, keepdims=True)
    picked = jnp.take(logits, draft_to_target, axis=1)
    probs = (jnp.exp(picked - peak) / total).astype(jnp.bfloat16)
    mass = jnp.sum(probs.astype(jnp.float32), axis=1)
    blocks = probs.reshape(N_DP, TOK_DEV, VD)
    mass_blocks = mass.reshape(N_DP, TOK_DEV)
    grads = []
    grad_head = jnp.zeros((D, VD), jnp.float32)
    for step in range(STEPS):
        shifted = jnp.concatenate([blocks[:, step:], jnp.zeros((N_DP, step, VD), jnp.bfloat16)], axis=1).reshape(TOKENS, VD)
        shifted_mass = jnp.concatenate([mass_blocks[:, step:], jnp.zeros((N_DP, step), jnp.float32)], axis=1).reshape(TOKENS)
        scores = jnp.dot(hidden[step], draft_head, preferred_element_type=jnp.float32)
        top = jnp.max(scores, axis=1, keepdims=True)
        expo = jnp.exp(scores - top)
        soft = expo / jnp.sum(expo, axis=1, keepdims=True)
        slopes = (LOSS_SCALE * STEP_DECAY ** step * (soft * shifted_mass[:, None] - shifted.astype(jnp.float32))).astype(jnp.bfloat16)
        grads.append(jnp.dot(slopes, draft_head.T, preferred_element_type=jnp.float32).astype(jnp.bfloat16))
        grad_head = grad_head + jnp.dot(hidden[step].T, slopes, preferred_element_type=jnp.float32)
    return jnp.stack(grads), grad_head
```

```python
import functools

import jax
import jax.numpy as jnp
from jax import lax
from jax.experimental import pallas as pl
from jax.experimental.pallas import tpu as pltpu
from jax.sharding import PartitionSpec as P

LOSS_SCALE = 256.0
STEP_DECAY = 0.8
MESH = pl.DeviceIdType.MESH
F32 = jnp.float32
BF16 = jnp.bfloat16
RING = 4
CORES = 2
LOW = -3.0e38


def ceil_to(value, unit):
    return (value + unit - 1) // unit * unit


def pick_kernel(slots, ids_ref, logits_ref, out_ref, stat_ref, place_ref, flipped, marks, tables):
    parts, block = ids_ref.shape
    tokens, shard = logits_ref.shape
    depth = flipped.shape[0]
    wide = ceil_to(block, 256)
    me = lax.axis_index("tensor")

    whole = shard // 256

    def flip(c, _):
        at = pl.multiple_of(c * 256, 256)
        flipped[pl.ds(at, 256), :] = logits_ref[:, pl.ds(at, 256)].T
        return 0

    lax.fori_loop(0, whole, flip, 0)
    rest = shard - whole * 256
    if rest:
        tail = jnp.concatenate(
            [logits_ref[:, whole * 256 :], jnp.full((tokens, 256 - rest), LOW, BF16)], axis=1
        )
        flipped[whole * 256 :, :] = tail.T

    rows = 256

    def peak_step(c, best):
        at = pl.multiple_of(c * rows, rows)
        part = flipped[pl.ds(at, rows), :].astype(F32).reshape(rows // 8, 8, tokens)
        return jnp.maximum(best, jnp.max(part, axis=0))

    best = lax.fori_loop(0, depth // rows, peak_step, jnp.full((8, tokens), LOW, F32))
    peak = jnp.max(best, axis=0, keepdims=True)

    def sum_step(c, acc):
        at = pl.multiple_of(c * rows, rows)
        part = jnp.exp(flipped[pl.ds(at, rows), :].astype(F32) - peak).reshape(rows // 8, 8, tokens)
        return acc + jnp.sum(part, axis=0)

    acc = lax.fori_loop(0, depth // rows, sum_step, jnp.zeros((8, tokens), F32))
    total = jnp.sum(acc, axis=0, keepdims=True)
    row = lax.broadcasted_iota(jnp.int32, (8, tokens), 0)
    stat_ref[...] = jnp.where(row == 0, peak, jnp.where(row == 1, total, 0.0))

    ids = jnp.concatenate([ids_ref[...], jnp.full((parts, wide - block), -1, jnp.int32)], axis=1)
    local = ids - me * shard
    mine = (local >= 0) & (local < shard)
    own = jnp.concatenate(
        [ids_ref[pl.ds(me, 1), :], jnp.full((1, wide - block), -1, jnp.int32)], axis=1
    )
    start = lax.broadcasted_iota(jnp.int32, (parts, wide), 0) * shard
    from_owner = (own >= start) & (own < start + shard)
    hits = jnp.concatenate([jnp.where(mine, 1.0, 0.0), jnp.where(from_owner, 1.0, 0.0)], axis=0)
    before = lax.broadcasted_iota(jnp.int32, (wide, wide), 0)
    after = lax.broadcasted_iota(jnp.int32, (wide, wide), 1)
    upper = jnp.where(before <= after, 1.0, 0.0).astype(BF16)
    ranks = jnp.dot(hits.astype(BF16), upper, preferred_element_type=F32) - 1.0
    owner = lax.broadcasted_iota(jnp.int32, (parts, wide), 0).astype(F32) * float(slots)
    place = jnp.sum(jnp.where(from_owner, owner + ranks[parts:], 0.0), axis=0, keepdims=True)
    place = jnp.where(own >= 0, place, -1.0)
    place_ref[...] = jnp.broadcast_to(place, (8, wide)).astype(jnp.int32)
    tables[0] = jnp.where(mine, ranks[:parts], -1.0)
    tables[1] = jnp.where(mine, local >> 8, 0).astype(F32)
    tables[2] = jnp.where(mine, local & 255, 0).astype(F32)

    def block_step(b, _):
        rank = tables[0, pl.ds(b, 1), :]
        high = jnp.broadcast_to(tables[1, pl.ds(b, 1), :], (128, wide)).astype(BF16)
        low = jnp.broadcast_to(tables[2, pl.ds(b, 1), :] , (128, wide)).astype(BF16)
        slot = lax.broadcasted_iota(jnp.int32, (slots, wide), 0).astype(F32)
        hot = jnp.where(slot == rank, 1.0, 0.0).astype(BF16)
        nt = (((1,), (1,)), ((), ()))
        used = lax.dot_general(hot, jnp.ones((128, wide), BF16), nt, preferred_element_type=F32)
        high_of = lax.dot_general(hot, high, nt, preferred_element_type=F32)
        low_of = lax.dot_general(hot, low, nt, preferred_element_type=F32)
        high_of = jnp.where(used > 0.5, high_of, -1.0)
        lane = lax.broadcasted_iota(jnp.int32, (slots, 128), 1).astype(F32)
        left = jnp.where(low_of == lane, 1.0, 0.0).astype(BF16)
        right = jnp.where(low_of == lane + 128.0, 1.0, 0.0).astype(BF16)
        high_of = high_of.astype(BF16)
        zero = jnp.zeros((slots, 128), BF16)
        for c in range(depth // 256):
            here = high_of == jnp.asarray(float(c), BF16)
            marks[:, c * 256 : c * 256 + 128] = jnp.where(here, left, zero)
            marks[:, c * 256 + 128 : c * 256 + 256] = jnp.where(here, right, zero)
        out_ref[b] = jnp.dot(marks[...], flipped[...], preferred_element_type=F32).astype(BF16)
        return 0

    lax.fori_loop(0, parts, block_step, 0)


def pick(ids, logits, slots):
    parts, block = ids.shape
    tokens, shard = logits.shape
    depth = ceil_to(shard, 256)
    wide = ceil_to(block, 256)
    vmem = pl.BlockSpec(memory_space=pltpu.VMEM)
    return pl.pallas_call(
        functools.partial(pick_kernel, slots),
        out_shape=(
            jax.ShapeDtypeStruct((parts, slots, tokens), BF16),
            jax.ShapeDtypeStruct((8, tokens), F32),
            jax.ShapeDtypeStruct((8, wide), jnp.int32),
        ),
        in_specs=[vmem, vmem],
        out_specs=(vmem, vmem, vmem),
        scratch_shapes=[
            pltpu.VMEM((depth, tokens), BF16),
            pltpu.VMEM((slots, depth), BF16),
            pltpu.VMEM((3, parts, wide), F32),
        ],
        compiler_params=pltpu.CompilerParams(vmem_limit_bytes=50 * 2**20),
        cost_estimate=pl.CostEstimate(
            flops=2 * parts * slots * depth * tokens, bytes_accessed=4 * tokens * shard, transcendentals=tokens * shard
        ),
        name="pick",
    )(ids, logits)


def as_column(rows):
    wide = jnp.broadcast_to(rows[0:1, :], (128, rows.shape[1]))
    return wide.T[:, 0:1]


def as_row(column):
    wide = jnp.broadcast_to(column, (column.shape[0], 128))
    return wide.T[0:1, :]


def tail_kernel(
    sizes,
    scores_ref,
    inc_ref,
    stat_ref,
    place_ref,
    ht_ref,
    w_ref,
    gh_ref,
    gw_ref,
    probs,
    slopes,
    h_peer,
    w_buf,
    terms,
    exch,
    x_out,
    x_far,
    x_in,
    p_out,
    p_far,
    p_in,
    q_out,
    q_far,
    q_in,
    p2_out,
    p2_far,
    p2_in,
    q2_out,
    q2_far,
    q2_in,
    ex_send,
    ex_recv,
    pair_send,
    pair_recv,
    w_sem,
    ring_send,
    ring_recv,
):
    steps, tokens, block, wide = sizes
    parts = RING * RING
    both = steps * tokens
    dp = lax.axis_index("dp")
    tensor = lax.axis_index("tensor")
    x, core = dp // CORES, dp % CORES
    z, y = tensor // RING, tensor % RING
    d = ht_ref.shape[0]
    sub = d // parts
    own_rows = d // (RING * CORES)
    half = own_rows // 2

    def x_peer(by):
        return (((x + by) % RING) * CORES + core, tensor)

    def z_peer(by):
        return (dp, ((z + by) % RING) * RING + y)

    def y_peer(by):
        return (dp, z * RING + (y + by) % RING)

    partner = (x * CORES + 1 - core, tensor)

    barrier = pltpu.get_barrier_semaphore()
    for i in range(1, parts):
        pl.semaphore_signal(barrier, inc=1, device_id=(dp, (tensor + i) % parts), device_id_type=MESH)
    pl.semaphore_signal(barrier, inc=1, device_id=partner, device_id_type=MESH)
    for by in (1, RING - 1):
        pl.semaphore_signal(barrier, inc=1, device_id=x_peer(by), device_id_type=MESH)
    pl.semaphore_wait(barrier, parts + 2)

    def remote(src, dst, send, recv, device):
        return pltpu.make_async_remote_copy(
            src_ref=src, dst_ref=dst, send_sem=send, recv_sem=recv, device_id=device, device_id_type=MESH
        )

    def exchange(turn):
        copies = []
        for i in range(1, parts):
            copies.append(
                remote(
                    exch.at[turn, tensor],
                    exch.at[turn, tensor],
                    ex_send.at[turn, i],
                    ex_recv.at[turn, i],
                    (dp, (tensor + i) % parts),
                )
            )
        for copy in copies:
            copy.start()
        return copies

    exch[0, tensor, :, 0:tokens] = stat_ref[...]
    exch[0, tensor, :, tokens:both] = stat_ref[...]
    first = exchange(0)

    pair = []
    for i in range(RING):
        rows = pl.multiple_of((i * CORES + 1 - core) * own_rows, own_rows)
        pair.append(
            remote(ht_ref.at[pl.ds(rows, own_rows)], h_peer.at[i], pair_send.at[i], pair_recv.at[i], partner)
        )
        pair[-1].start()

    w_rows = w_buf.shape[1]

    def w_copy(i, slot):
        rows = pl.multiple_of(i * w_rows, w_rows)
        return pltpu.make_async_copy(w_ref.at[pl.ds(rows, w_rows)], w_buf.at[slot], w_sem.at[slot])

    w_copy(0, 0).start()
    w_copy(1, 1).start()

    band = 64
    lanes = lax.broadcasted_iota(jnp.int32, (band, block), 1)

    top = jnp.concatenate([jnp.max(scores_ref[pl.ds(i, 128), :], axis=1, keepdims=True) for i in range(0, both, 128)], axis=0)
    mass_sum = jnp.concatenate(
        [
            jnp.sum(jnp.exp(scores_ref[pl.ds(i, 128), :] - top[i : i + 128]), axis=1, keepdims=True)
            for i in range(0, both, 128)
        ],
        axis=0,
    )
    top_row = as_row(top)
    sum_row = as_row(mass_sum)

    slots_all = inc_ref.shape[0]
    place = place_ref[0:1, :]
    n_tile = 512
    for n in range(0, wide, n_tile):
        place_n = place[:, n : n + n_tile]
        row = lax.broadcasted_iota(jnp.int32, (256, n_tile), 0)

        def pick_step(c, acc):
            at = pl.multiple_of(c * 256, 256)
            hot = jnp.where(row + at == place_n, 1.0, 0.0).astype(BF16)
            return acc + lax.dot_general(
                inc_ref[pl.ds(at, 256), :], hot, (((0,), (0,)), ((), ())), preferred_element_type=F32
            )

        probs[:, n : n + n_tile] = lax.fori_loop(
            0, slots_all // 256, pick_step, jnp.zeros((tokens, n_tile), F32)
        )

    for copy in first:
        copy.wait()
    peaks = [exch[0, i, 0:1, :] for i in range(parts)]
    t_peak = functools.reduce(jnp.maximum, peaks)
    t_total = sum(exch[0, i, 1:2, :] * jnp.exp(peaks[i] - t_peak) for i in range(parts))
    t_peak_c = as_column(t_peak[:, 0:tokens])
    t_total_c = as_column(t_total[:, 0:tokens])
    masses = []
    for i in range(0, tokens, band):
        value = jnp.exp(probs[i : i + band, :] - t_peak_c[i : i + band]) / t_total_c[i : i + band]
        inside = lax.broadcasted_iota(jnp.int32, (band, wide), 1) < block
        value = jnp.where(inside, value, 0.0).astype(BF16).astype(F32)
        probs[i : i + band, :] = value
        masses.append(jnp.sum(value, axis=1, keepdims=True))
    mass_row = as_row(jnp.concatenate(masses, axis=0))

    kind = lax.broadcasted_iota(jnp.int32, (8, both), 0)
    mass_row = jnp.concatenate([mass_row] * steps, axis=1)
    exch[1, tensor] = jnp.where(
        kind == 0, top_row, jnp.where(kind == 1, sum_row, jnp.where(kind == 2, mass_row, 0.0))
    )
    second = exchange(1)
    for copy in second:
        copy.wait()
    tops = [exch[1, i, 0:1, :] for i in range(parts)]
    top_all = functools.reduce(jnp.maximum, tops)
    sum_all = sum(exch[1, i, 1:2, :] * jnp.exp(tops[i] - top_all) for i in range(parts))
    mass_all = sum(exch[1, i, 2:3, :] for i in range(parts))
    top_c = as_column(top_all)
    sum_c = as_column(sum_all)
    mass_c = as_column(mass_all[:, 0:tokens])

    for step in range(steps):
        for i in range(0, tokens, band):
            r = step * tokens + i
            soft = jnp.exp(scores_ref[r : r + band, :] - top_c[r : r + band]) / sum_c[r : r + band]
            if step == 0:
                shifted = probs[i : i + band, 0:block]
                mass = mass_c[i : i + band]
            else:
                got = min(band, tokens - i - step)
                shifted = probs[i + step : i + step + got, 0:block]
                mass = mass_c[i + step : i + step + got]
                if got < band:
                    shifted = jnp.concatenate([shifted, jnp.zeros((band - got, block), F32)], axis=0)
                    mass = jnp.concatenate([mass, jnp.zeros((band - got, 1), F32)], axis=0)
            slope = LOSS_SCALE * STEP_DECAY**step * (soft * mass - shifted)
            slope = jnp.concatenate([slope, jnp.zeros((band, wide - block), F32)], axis=1)
            slopes[0, r : r + band, :] = slope.astype(BF16)

    swap = remote(slopes.at[0], slopes.at[1], pair_send.at[RING], pair_recv.at[RING], partner)
    swap.start()
    for copy in pair:
        copy.wait()
    swap.wait()

    piece = 160

    def head_part(by, rows):
        chip = (x + by) % RING
        at = pl.multiple_of((chip * CORES + core) * own_rows + rows, piece)
        mine = jnp.dot(ht_ref[pl.ds(at, piece), :], slopes[0], preferred_element_type=F32)
        return mine + jnp.dot(
            h_peer[chip, pl.ds(pl.multiple_of(rows, piece), piece), :], slopes[1], preferred_element_type=F32
        )

    def link(n, src, dst, device):
        return remote(src, dst, ring_send.at[n], ring_recv.at[n], device)

    count = half // piece

    def fill(out, by, first_row, rows):
        def go(i, _):
            at = pl.multiple_of(rows + i * piece, piece)
            to = pl.multiple_of(first_row + i * piece, piece)
            out[pl.ds(to, piece), :] = head_part(by, at).astype(BF16)
            return 0

        lax.fori_loop(0, count, go, 0)

    fill(x_out.at[0], 2, 0, 0)
    far_r = link(0, x_out.at[0], x_far.at[0], x_peer(1))
    far_r.start()
    fill(x_out.at[1], 2, 0, half)
    far_l = link(1, x_out.at[1], x_far.at[1], x_peer(RING - 1))
    far_l.start()
    fill(x_out.at[3], 1, 0, half)
    free_r = link(2, x_out.at[3], x_in.at[1], x_peer(1))
    free_r.start()
    fill(x_out.at[4], RING - 1, 0, 0)
    free_l = link(3, x_out.at[4], x_in.at[2], x_peer(RING - 1))
    free_l.start()

    per = w_rows // sub

    def term_step(i, _):
        slot = i % 2
        w_copy(i, slot).wait()
        for s in range(per):
            terms[i * per + s] = lax.dot_general(
                w_buf[slot, s * sub : (s + 1) * sub, :],
                slopes[0, :, 0:block],
                (((1,), (1,)), ((), ())),
                preferred_element_type=F32,
            )

        @pl.when(i + 2 < d // w_rows)
        def _():
            w_copy(i + 2, slot).start()

        return 0

    lax.fori_loop(0, d // w_rows, term_step, 0)

    pair_of = RING // 2
    p_at, q_at = pl.ds(0, tokens), pl.ds(tokens, tokens)

    def p_term(by, n):
        return terms[((z + by) % RING) * RING + n, :, p_at]

    def q_term(by, n):
        return terms[n * RING + (y + by) % RING, :, q_at]

    def start_first(term, out, far, into, peer, base):
        def put(slot, by, first, extra=None):
            for n in range(pair_of):
                value = term(by, first + n)
                if extra is not None:
                    value = value + extra[n].astype(F32)
                out[slot, n] = value.astype(BF16)

        put(0, 2, 0)
        a = link(base, out.at[0], far.at[0], peer(1))
        a.start()
        put(1, 2, pair_of)
        b = link(base + 1, out.at[1], far.at[1], peer(RING - 1))
        b.start()
        put(3, 1, pair_of)
        c = link(base + 2, out.at[3], into.at[1], peer(1))
        c.start()
        put(4, RING - 1, 0)
        e = link(base + 3, out.at[4], into.at[2], peer(RING - 1))
        e.start()

        def later():
            a.wait()
            put(2, 1, 0, far.at[0])
            f = link(base + 4, out.at[2], into.at[0], peer(1))
            f.start()
            b.wait()
            put(5, RING - 1, pair_of, far.at[1])
            g = link(base + 5, out.at[5], into.at[3], peer(RING - 1))
            g.start()

            def done():
                for copy in (c, e, f, g):
                    copy.wait()

            return done

        return later

    p_later = start_first(p_term, p_out, p_far, p_in, z_peer, 6)
    q_later = start_first(q_term, q_out, q_far, q_in, y_peer, 12)
    p_done = p_later()
    q_done = q_later()

    far_r.wait()

    def add_right(i, _):
        at = pl.multiple_of(i * piece, piece)
        value = head_part(1, at) + x_far[0, pl.ds(at, piece), :].astype(F32)
        x_out[2, pl.ds(at, piece), :] = value.astype(BF16)
        return 0

    lax.fori_loop(0, count, add_right, 0)
    dep_r = link(4, x_out.at[2], x_in.at[0], x_peer(1))
    dep_r.start()
    far_l.wait()

    def add_left(i, _):
        at = pl.multiple_of(i * piece, piece)
        value = head_part(RING - 1, half + at) + x_far[1, pl.ds(at, piece), :].astype(F32)
        x_out[5, pl.ds(at, piece), :] = value.astype(BF16)
        return 0

    lax.fori_loop(0, count, add_left, 0)
    dep_l = link(5, x_out.at[5], x_in.at[3], x_peer(RING - 1))
    dep_l.start()

    p_done()
    for n in range(RING):
        got = p_in[n // pair_of, n % pair_of].astype(F32) + p_in[2 + n // pair_of, n % pair_of].astype(F32)
        mine = z * RING + n
        terms[mine, :, p_at] = terms[mine, :, p_at] + got
    q_done()
    for n in range(RING):
        got = q_in[n // pair_of, n % pair_of].astype(F32) + q_in[2 + n // pair_of, n % pair_of].astype(F32)
        mine = n * RING + y
        terms[mine, :, q_at] = terms[mine, :, q_at] + got

    cut = sub // 2

    def start_second(lane, index, out, far, into, peer, base):
        def put(slot, by, first, extra=None):
            value = terms[index(by), first : first + cut, lane]
            if extra is not None:
                value = value + extra[...].astype(F32)
            out[slot] = value.astype(BF16)

        put(0, 2, 0)
        a = link(base, out.at[0], far.at[0], peer(1))
        a.start()
        put(1, 2, cut)
        b = link(base + 1, out.at[1], far.at[1], peer(RING - 1))
        b.start()
        put(3, 1, cut)
        c = link(base + 2, out.at[3], into.at[1], peer(1))
        c.start()
        put(4, RING - 1, 0)
        e = link(base + 3, out.at[4], into.at[2], peer(RING - 1))
        e.start()

        def later():
            a.wait()
            put(2, 1, 0, far.at[0])
            f = link(base + 4, out.at[2], into.at[0], peer(1))
            f.start()
            b.wait()
            put(5, RING - 1, cut, far.at[1])
            g = link(base + 5, out.at[5], into.at[3], peer(RING - 1))
            g.start()

            def done():
                for copy in (c, e, f, g):
                    copy.wait()
                for n in range(2):
                    value = terms[tensor, n * cut : (n + 1) * cut, lane]
                    value = value + into[n].astype(F32) + into[2 + n].astype(F32)
                    gh_ref[n * cut : (n + 1) * cut, lane] = value.astype(BF16)

            return done

        return later

    p2_later = start_second(p_at, lambda by: z * RING + (y + by) % RING, p2_out, p2_far, p2_in, y_peer, 18)
    q2_later = start_second(q_at, lambda by: ((z + by) % RING) * RING + y, q2_out, q2_far, q2_in, z_peer, 24)
    p2_done = p2_later()
    q2_done = q2_later()

    def own_step(i, _):
        at = pl.multiple_of(i * piece, piece)
        gw_ref[pl.ds(at, piece), :] = head_part(0, at)[:, 0:block]
        return 0

    lax.fori_loop(0, own_rows // piece, own_step, 0)
    p2_done()
    q2_done()

    for copy in (free_r, free_l, dep_r, dep_l):
        copy.wait()
    for h in range(2):

        def last_step(i, _, h=h):
            at = pl.multiple_of(i * 32, 32)
            to = pl.multiple_of(h * half + i * 32, 32)
            got = x_in[h, pl.ds(at, 32), :].astype(F32) + x_in[2 + h, pl.ds(at, 32), :].astype(F32)
            gw_ref[pl.ds(to, 32), :] = gw_ref[pl.ds(to, 32), :] + got[:, 0:block]
            return 0

        lax.fori_loop(0, half // 32, last_step, 0)


def tail(scores, incoming, stat, place, ht, w, tokens):
    both, block = scores.shape
    steps = both // tokens
    d = ht.shape[0]
    parts = RING * RING
    sub = d // parts
    own_rows = d // (RING * CORES)
    half = own_rows // 2
    wide = ceil_to(block, 256)
    vmem = pl.BlockSpec(memory_space=pltpu.VMEM)
    ring_x = [(6, half, wide), (2, half, wide), (4, half, wide)]
    ring_1 = [(6, 2, sub, tokens), (2, 2, sub, tokens), (4, 2, sub, tokens)]
    ring_2 = [(6, sub // 2, tokens), (2, sub // 2, tokens), (4, sub // 2, tokens)]
    return pl.pallas_call(
        functools.partial(tail_kernel, (steps, tokens, block, wide)),
        out_shape=(
            jax.ShapeDtypeStruct((sub, both), BF16),
            jax.ShapeDtypeStruct((own_rows, block), F32),
        ),
        in_specs=[vmem, vmem, vmem, vmem, vmem, pl.BlockSpec(memory_space=pl.ANY)],
        out_specs=(vmem, vmem),
        scratch_shapes=[
            pltpu.VMEM((tokens, wide), F32),
            pltpu.VMEM((2, both, wide), BF16),
            pltpu.VMEM((RING, own_rows, both), BF16),
            pltpu.VMEM((2, 2 * sub, block), BF16),
            pltpu.VMEM((parts, sub, both), F32),
            pltpu.VMEM((2, parts, 8, both), F32),
        ]
        + [pltpu.VMEM(shape, BF16) for shape in ring_x + ring_1 + ring_1 + ring_2 + ring_2]
        + [
            pltpu.SemaphoreType.DMA((2, parts)),
            pltpu.SemaphoreType.DMA((2, parts)),
            pltpu.SemaphoreType.DMA((RING + 1,)),
            pltpu.SemaphoreType.DMA((RING + 1,)),
            pltpu.SemaphoreType.DMA((2,)),
            pltpu.SemaphoreType.DMA((30,)),
            pltpu.SemaphoreType.DMA((30,)),
        ],
        compiler_params=pltpu.CompilerParams(
            collective_id=3, has_side_effects=True, vmem_limit_bytes=63 * 2**20
        ),
        name="tail",
    )(scores, incoming, stat, place, ht, w)


def per_device(hidden, draft_head, target_logits, draft_to_target):
    parts = lax.axis_size("tensor")
    steps, tokens, width = hidden.shape
    block = draft_to_target.shape[0] // parts
    heavy = block // 8
    bound = heavy + (block - heavy + parts - 1) // parts
    slots = ceil_to(bound, 16)

    flat = hidden.reshape(steps * tokens, width).T
    ht = lax.all_gather(flat, "tensor", axis=0, tiled=True)
    picked, stat, place = pick(draft_to_target.reshape(parts, block), target_logits, slots)
    incoming = lax.all_to_all(picked, "tensor", split_axis=0, concat_axis=0, tiled=True)
    scores = lax.dot_general(ht, draft_head, (((0,), (0,)), ((), ())), preferred_element_type=F32)
    gh, gw = tail(scores, incoming.reshape(parts * slots, tokens), stat, place, ht, draft_head, tokens)
    return gh.T.reshape(steps, tokens, width), gw


def solution(mesh):
    in_specs = (P(None, "dp", "tensor"), P(None, "tensor"), P("dp", "tensor"), P())
    out_specs = (P(None, "dp", "tensor"), P("dp", "tensor"))
    return jax.shard_map(
        per_device, mesh=mesh, in_specs=in_specs, out_specs=out_specs, check_vma=False
    )
```

```python
import functools

import jax
import jax.numpy as jnp
from jax import lax
from jax.experimental import pallas as pl
from jax.experimental.pallas import tpu as pltpu
from jax.sharding import PartitionSpec as P

LOSS_SCALE = 256.0
STEP_DECAY = 0.8
MESH = pl.DeviceIdType.MESH
F32 = jnp.float32
BF16 = jnp.bfloat16
I32 = jnp.int32
RING = 4
CORES = 2
PARTS = RING * RING
LOW = -3.0e38
NT = (((1,), (1,)), ((), ()))


def ceil_to(value, unit):
    return (value + unit - 1) // unit * unit


def places():
    dp = lax.axis_index("dp")
    tensor = lax.axis_index("tensor")
    x, core = dp // CORES, dp % CORES
    z, y = tensor // RING, tensor % RING
    return dp, tensor, x, core, z, y


def remote(src, dst, send, recv, device):
    return pltpu.make_async_remote_copy(
        src_ref=src, dst_ref=dst, send_sem=send, recv_sem=recv, device_id=device, device_id_type=MESH
    )


def pieces_of(rows):
    half = rows // 2
    first = ceil_to(half // 2, 16)
    return [(0, first), (first, half - first), (half, first), (half + first, half - first)]


def front_kernel(
    sizes,
    hid_ref,
    ids_ref,
    logits_ref,
    w_ref,
    sl_ref,
    hn_ref,
    ht,
    h_peer,
    w_buf,
    source,
    picked,
    outgoing,
    incoming,
    expo,
    probs,
    rank_v,
    tab_v,
    place_v,
    ex1,
    ex2,
    tab_s,
    place_s,
    ag_send,
    ag_recv,
    a2a_send,
    a2a_recv,
    ex_send,
    ex_recv,
    pair_send,
    pair_recv,
    w_sem,
    s_sem,
):
    steps, tokens, block, rows, slots = sizes
    shard = logits_ref.shape[0]
    sub = hid_ref.shape[1]
    both = steps * tokens
    wide = ceil_to(block, 256)
    lane_parts = tokens // 128
    dp, tensor, x, core, z, y = places()
    partner = (x * CORES + 1 - core, tensor)

    def z_peer(by):
        return (dp, ((z + by) % RING) * RING + y)

    def y_peer(by):
        return (dp, z * RING + (y + by) % RING)

    def group_peer(i):
        return (dp, (tensor + i) % PARTS)

    chunk = w_buf.shape[2]

    def w_copy(i):
        return pltpu.make_async_copy(w_ref.at[:, pl.ds(i * chunk, chunk)], w_buf.at[i % 2], w_sem.at[i % 2])

    w_copy(0).start()
    w_copy(1).start()
    for s in range(steps):
        ht[s, z, y] = hid_ref[s]

    barrier = pltpu.get_barrier_semaphore()
    for i in range(1, PARTS):
        pl.semaphore_signal(barrier, inc=1, device_id=group_peer(i), device_id_type=MESH)
    pl.semaphore_signal(barrier, inc=1, device_id=partner, device_id_type=MESH)
    pl.semaphore_wait(barrier, PARTS)

    def gather_ring(half, at, peer, base):
        right, left = (at + 1) % RING, (at + RING - 1) % RING

        def copy(n, r, h, by):
            ref = half(r, h)
            return remote(ref, ref, ag_send.at[base + n], ag_recv.at[base + n], peer(by))

        r1 = copy(0, at, 0, 1)
        l1 = copy(1, at, 1, RING - 1)
        r2 = copy(2, at, 1, 1)
        l2 = copy(3, at, 0, RING - 1)
        for c in (r1, l1, r2, l2):
            c.start()

        def pass_on():
            r1.wait()
            r3 = copy(4, left, 0, 1)
            r3.start()
            l1.wait()
            l3 = copy(5, right, 1, RING - 1)
            l3.start()

            def finish():
                for c in (r2, l2, r3, l3):
                    c.wait()

            return finish

        return pass_on

    def half_rows(s, at_z, at_y, h):
        return ht.at[s, at_z, at_y, pl.ds(h * (sub // 2), sub // 2)]

    two = RING // 2
    p1 = gather_ring(lambda r, h: half_rows(0, z, r, h), y, y_peer, 0)
    q1 = gather_ring(lambda r, h: half_rows(1, r, y, h), z, z_peer, 6)

    ids = jnp.concatenate([ids_ref[...], jnp.full((PARTS, wide - block), -1, I32)], axis=1)
    local = ids - tensor * shard
    mine = (local >= 0) & (local < shard)
    own = jnp.sum(jnp.where(lax.broadcasted_iota(I32, (PARTS, wide), 0) == tensor, ids, 0), axis=0, keepdims=True)
    start = lax.broadcasted_iota(I32, (PARTS, wide), 0) * shard
    from_owner = (own >= start) & (own < start + shard)
    hits = jnp.concatenate([jnp.where(mine, 1.0, 0.0), jnp.where(from_owner, 1.0, 0.0)], axis=0)
    before = lax.broadcasted_iota(I32, (256, 256), 0)
    after = lax.broadcasted_iota(I32, (256, 256), 1)
    upper = jnp.where(before <= after, 1.0, 0.0).astype(BF16)
    seen = jnp.full((2 * PARTS, 1), -1.0, F32)
    rank_list = []
    for n in range(wide // 256):
        part = hits[:, n * 256 : (n + 1) * 256]
        rank_list.append(jnp.dot(part.astype(BF16), upper, preferred_element_type=F32) + seen)
        seen = seen + jnp.sum(part, axis=1, keepdims=True)
    ranks = jnp.concatenate(rank_list, axis=1)
    owner = lax.broadcasted_iota(I32, (PARTS, wide), 0).astype(F32) * float(slots)
    place = jnp.sum(jnp.where(from_owner, owner + ranks[PARTS:], 0.0), axis=0, keepdims=True)
    place_v[...] = jnp.broadcast_to(place, (8, wide)).astype(I32)
    rank_v[0] = jnp.where(mine, ranks[:PARTS], -1.0)
    rank_v[1] = jnp.where(mine, local - (local & 255), 0).astype(F32)
    rank_v[2] = jnp.where(mine, local & 255, 0).astype(F32)
    to_place = pltpu.make_async_copy(place_v, place_s, s_sem.at[0])
    to_place.start()

    p1_end = p1()
    q1_end = q1()

    slot = lax.broadcasted_iota(I32, (tab_v.shape[1], wide), 0).astype(F32)
    kind = lax.broadcasted_iota(I32, (8, wide), 0)

    def table_step(b, _):
        rank = rank_v[0, pl.ds(b, 1), :]
        info = jnp.where(kind == 0, rank_v[1, pl.ds(b, 1), :], jnp.where(kind == 1, rank_v[2, pl.ds(b, 1), :], 0.0))
        hot = jnp.where(slot == rank, 1.0, 0.0).astype(BF16)
        got = lax.dot_general(info.astype(BF16), hot, NT, preferred_element_type=F32)
        tab_v[pl.ds(b, 1), :] = (got[0:1, :] + got[1:2, :]).astype(I32)
        return 0

    lax.fori_loop(0, PARTS, table_step, 0)
    to_tab = pltpu.make_async_copy(tab_v, tab_s, s_sem.at[1])
    to_tab.start()

    p1_end()
    q1_end()
    p2 = gather_ring(lambda r, h: ht.at[0, r, pl.ds(h * two, two)], z, z_peer, 12)
    q2 = gather_ring(lambda r, h: ht.at[1, pl.ds(h * two, two), r], y, y_peer, 18)

    band = 32
    whole = shard // band

    def widen(at, size, best):
        part = logits_ref[pl.ds(at, size), :].astype(F32)
        for c in range(lane_parts):
            source[c, pl.ds(at, size), :] = part[:, c * 128 : (c + 1) * 128]
        return jnp.maximum(best, jnp.max(part.reshape(size // 8, 8, tokens), axis=0))

    best = lax.fori_loop(
        0, whole, lambda i, m: widen(pl.multiple_of(i * band, band), band, m), jnp.full((8, tokens), LOW, F32)
    )
    if shard > whole * band:
        best = widen(whole * band, shard - whole * band, best)
    peak_here = jnp.max(best, axis=0, keepdims=True)

    def sum_exp(at, size, acc):
        part = jnp.exp(logits_ref[pl.ds(at, size), :].astype(F32) - peak_here)
        return acc + jnp.sum(part.reshape(size // 8, 8, tokens), axis=0)

    acc = lax.fori_loop(
        0, whole, lambda i, a: sum_exp(pl.multiple_of(i * band, band), band, a), jnp.zeros((8, tokens), F32)
    )
    if shard > whole * band:
        acc = sum_exp(whole * band, shard - whole * band, acc)
    total_here = jnp.sum(acc, axis=0, keepdims=True)
    row8 = lax.broadcasted_iota(I32, (8, tokens), 0)
    ex1[tensor] = jnp.where(row8 == 0, peak_here, jnp.where(row8 == 1, total_here, 0.0))
    first = [
        remote(ex1.at[tensor], ex1.at[tensor], ex_send.at[0, i], ex_recv.at[0, i], group_peer(i))
        for i in range(1, PARTS)
    ]
    for copy in first:
        copy.start()

    to_tab.wait()
    to_place.wait()

    def pick(index_of, count):
        def go(i, _):
            for r in range(16):
                j = i * 16 + r
                at = jnp.clip(index_of(j), 0, source.shape[1] - 1)
                for c in range(lane_parts):
                    picked[c, pl.ds(j, 1), :] = source[c, pl.ds(at, 1), :]
            return 0

        lax.fori_loop(0, count // 16, go, 0)

    def joined(at, size):
        return jnp.concatenate([picked[c, pl.ds(at, size), :] for c in range(lane_parts)], axis=1)

    def sent(i):
        to = (tensor + i) % PARTS
        return remote(outgoing.at[to], incoming.at[tensor], a2a_send.at[i], a2a_recv.at[i], (dp, to))

    def send_step(i, _):
        to = (tensor + i) % PARTS
        pick(lambda j: tab_s[to, j], slots)
        outgoing[to] = joined(0, slots).astype(BF16)
        sent(i).start()
        return 0

    lax.fori_loop(1, two * RING, send_step, 0)
    p2_end = p2()
    q2_end = q2()
    lax.fori_loop(two * RING, PARTS, send_step, 0)
    pick(lambda j: tab_s[tensor, j], slots)
    incoming[tensor] = joined(0, slots).astype(BF16)

    p2_end()
    q2_end()
    swap_h = remote(
        ht.at[:, :, pl.ds((1 - core) * CORES, CORES)], h_peer, pair_send.at[0], pair_recv.at[0], partner
    )
    swap_h.start()

    pieces = PARTS * sub // chunk
    each = chunk // sub
    expo[...] = jnp.zeros((rows, both), F32)

    def score_step(i, _):
        w_copy(i).wait()
        for s in range(steps):
            at = i * each
            h = ht[s, at // RING, pl.ds(at % RING, each)].reshape(chunk, tokens)
            lanes = slice(s * tokens, (s + 1) * tokens)
            expo[0:block, lanes] += jnp.dot(w_buf[i % 2], h, preferred_element_type=F32)

        @pl.when(i + 2 < pieces)
        def _():
            w_copy(i + 2).start()

        return 0

    lax.fori_loop(0, pieces, score_step, 0)
    if rows > block:
        expo[block:rows, :] = jnp.full((rows - block, both), LOW, F32)

    def top_step(i, m):
        at = pl.multiple_of(i * band, band)
        return jnp.maximum(m, jnp.max(expo[pl.ds(at, band), :].reshape(band // 8, 8, both), axis=0))

    top = lax.fori_loop(0, rows // band, top_step, jnp.full((8, both), LOW, F32))
    top = jnp.max(top, axis=0, keepdims=True)

    def exp_step(i, a):
        at = pl.multiple_of(i * band, band)
        value = jnp.exp(expo[pl.ds(at, band), :] - top)
        expo[pl.ds(at, band), :] = value
        return a + jnp.sum(value.reshape(band // 8, 8, both), axis=0)

    weight = lax.fori_loop(0, rows // band, exp_step, jnp.zeros((8, both), F32))
    weight = jnp.sum(weight, axis=0, keepdims=True)

    own_rows = CORES * sub
    for i in range(RING):
        for s in range(steps):
            part = ht[s, i, pl.ds(core * CORES, CORES)].reshape(own_rows, tokens)
            hn_ref[i, s * tokens : (s + 1) * tokens, :] = part.T
    swap_h.wait()
    for i in range(RING):
        for s in range(steps):
            part = h_peer[s, i].reshape(own_rows, tokens)
            hn_ref[i, both + s * tokens : both + (s + 1) * tokens, :] = part.T

    for copy in first:
        copy.wait()
    peaks = [ex1[i, 0:1, :] for i in range(PARTS)]
    peak = functools.reduce(jnp.maximum, peaks)
    total = sum(ex1[i, 1:2, :] * jnp.exp(peaks[i] - peak) for i in range(PARTS))

    def arrived(i, _):
        sent(i).wait()
        return 0

    lax.fori_loop(1, PARTS, arrived, 0)

    def widen_in(i, _):
        part = incoming[i].astype(F32)
        for c in range(lane_parts):
            source[c, pl.ds(pl.multiple_of(i * slots, 16), slots), :] = part[:, c * 128 : (c + 1) * 128]
        return 0

    lax.fori_loop(0, PARTS, widen_in, 0)
    pick(lambda j: place_s[0, j], rows)

    def prob_step(i, a):
        at = pl.multiple_of(i * band, band)
        value = jnp.exp(joined(at, band) - peak) / total
        inside = lax.broadcasted_iota(I32, (band, tokens), 0) + at < block
        value = jnp.where(inside, value, 0.0).astype(BF16).astype(F32)
        probs[pl.ds(at, band), :] = value
        return a + jnp.sum(value.reshape(band // 8, 8, tokens), axis=0)

    mass_here = lax.fori_loop(0, rows // band, prob_step, jnp.zeros((8, tokens), F32))
    mass_here = jnp.sum(mass_here, axis=0, keepdims=True)

    row8 = lax.broadcasted_iota(I32, (8, both), 0)
    mass_wide = jnp.concatenate([mass_here] * steps, axis=1)
    ex2[tensor] = jnp.where(row8 == 0, top, jnp.where(row8 == 1, weight, jnp.where(row8 == 2, mass_wide, 0.0)))
    second = [
        remote(ex2.at[tensor], ex2.at[tensor], ex_send.at[1, i], ex_recv.at[1, i], group_peer(i))
        for i in range(1, PARTS)
    ]
    for copy in second:
        copy.start()
    for copy in second:
        copy.wait()
    tops = [ex2[i, 0:1, :] for i in range(PARTS)]
    top_all = functools.reduce(jnp.maximum, tops)
    weight_all = sum(ex2[i, 1:2, :] * jnp.exp(tops[i] - top_all) for i in range(PARTS))
    mass = sum(ex2[i, 2:3, 0:tokens] for i in range(PARTS))

    def shift(value, step):
        if step == 0:
            return value
        lane = lax.broadcasted_iota(I32, value.shape, 1)
        return jnp.where(lane < tokens - step, pltpu.roll(value, tokens - step, 1), 0.0)

    factor = jnp.exp(top - top_all) / weight_all
    scales = [LOSS_SCALE * STEP_DECAY**s for s in range(steps)]
    coefs = []
    for s in range(steps):
        moved = shift(jnp.broadcast_to(mass, (8, tokens)), s)[0:1, :]
        coefs.append(scales[s] * moved * factor[:, s * tokens : (s + 1) * tokens])

    def slope_step(i, _):
        at = pl.multiple_of(i * 16, 16)
        prob = probs[pl.ds(at, 16), :]
        for s in range(steps):
            value = expo[pl.ds(at, 16), s * tokens : (s + 1) * tokens] * coefs[s] - scales[s] * shift(prob, s)
            sl_ref[pl.ds(at, 16), s * tokens : (s + 1) * tokens] = value.astype(BF16)
        return 0

    swaps = []
    for n, (at, size) in enumerate(pieces_of(rows)):
        lax.fori_loop(at // 16, (at + size) // 16, slope_step, 0)
        swaps.append(
            remote(
                sl_ref.at[pl.ds(at, size), pl.ds(0, both)],
                sl_ref.at[pl.ds(at, size), pl.ds(both, both)],
                pair_send.at[1 + n],
                pair_recv.at[1 + n],
                partner,
            )
        )
        swaps[-1].start()
    for copy in swaps:
        copy.wait()


def front(hid, ids, logits, w, slots):
    steps, sub, tokens = hid.shape
    parts, block = ids.shape
    shard = logits.shape[0]
    both = steps * tokens
    rows = ceil_to(block, 32)
    wide = ceil_to(block, 256)
    depth = ceil_to(max(shard, parts * slots), 32)
    vmem = pl.BlockSpec(memory_space=pltpu.VMEM)
    return pl.pallas_call(
        functools.partial(front_kernel, (steps, tokens, block, rows, slots)),
        out_shape=(
            jax.ShapeDtypeStruct((rows, CORES * both), BF16),
            jax.ShapeDtypeStruct((RING, CORES * both, CORES * sub), BF16),
        ),
        in_specs=[vmem, vmem, vmem, pl.BlockSpec(memory_space=pl.ANY)],
        out_specs=(vmem, vmem),
        scratch_shapes=[
            pltpu.VMEM((steps, RING, RING, sub, tokens), BF16),
            pltpu.VMEM((steps, RING, CORES, sub, tokens), BF16),
            pltpu.VMEM((2, block, 2 * sub), BF16),
            pltpu.VMEM((tokens // 128, depth, 128), F32),
            pltpu.VMEM((tokens // 128, ceil_to(max(rows, slots), 16), 128), F32),
            pltpu.VMEM((parts, slots, tokens), BF16),
            pltpu.VMEM((parts, slots, tokens), BF16),
            pltpu.VMEM((rows, both), F32),
            pltpu.VMEM((rows, tokens), F32),
            pltpu.VMEM((3, parts, wide), F32),
            pltpu.VMEM((parts, ceil_to(slots, 128)), I32),
            pltpu.VMEM((8, wide), I32),
            pltpu.VMEM((parts, 8, tokens), F32),
            pltpu.VMEM((parts, 8, both), F32),
            pltpu.SMEM((parts, ceil_to(slots, 128)), I32),
            pltpu.SMEM((8, wide), I32),
            pltpu.SemaphoreType.DMA((24,)),
            pltpu.SemaphoreType.DMA((24,)),
            pltpu.SemaphoreType.DMA((parts,)),
            pltpu.SemaphoreType.DMA((parts,)),
            pltpu.SemaphoreType.DMA((2, parts)),
            pltpu.SemaphoreType.DMA((2, parts)),
            pltpu.SemaphoreType.DMA((5,)),
            pltpu.SemaphoreType.DMA((5,)),
            pltpu.SemaphoreType.DMA((2,)),
            pltpu.SemaphoreType.DMA((2,)),
        ],
        compiler_params=pltpu.CompilerParams(
            collective_id=2, has_side_effects=True, vmem_limit_bytes=62 * 2**20
        ),
        name="front",
    )(hid, ids, logits, w)


def sums_kernel(
    sizes,
    sl_ref,
    hn_ref,
    w_ref,
    gh_ref,
    gw_ref,
    flat,
    w_buf,
    terms,
    x_out,
    x_far,
    x_in,
    p_out,
    p_far,
    p_in,
    q_out,
    q_far,
    q_in,
    p2_out,
    p2_far,
    p2_in,
    q2_out,
    q2_far,
    q2_in,
    w_sem,
    ring_send,
    ring_recv,
):
    steps, tokens, block = sizes
    rows = sl_ref.shape[0]
    both = steps * tokens
    dp, tensor, x, core, z, y = places()
    sub = gh_ref.shape[1]
    chunk = w_buf.shape[2]

    def x_peer(by):
        return (((x + by) % RING) * CORES + core, tensor)

    def z_peer(by):
        return (dp, ((z + by) % RING) * RING + y)

    def y_peer(by):
        return (dp, z * RING + (y + by) % RING)

    per = RING * sub // chunk
    count = RING * per

    def w_row(i):
        order = (2, 1, RING - 1, 0)[i // per]
        return ((z + order) % RING) * per + i % per

    def w_copy(i):
        at = pl.multiple_of(w_row(i) * chunk, chunk)
        return pltpu.make_async_copy(w_ref.at[:, pl.ds(at, chunk)], w_buf.at[i % 2], w_sem.at[i % 2])

    w_copy(0).start()
    w_copy(1).start()

    barrier = pltpu.get_barrier_semaphore()
    for peer in (x_peer, y_peer, z_peer):
        for by in (1, RING - 1):
            pl.semaphore_signal(barrier, inc=1, device_id=peer(by), device_id_type=MESH)
    pl.semaphore_wait(barrier, 6)

    def link(n, src, dst, device):
        return remote(src, dst, ring_send.at[n], ring_recv.at[n], device)

    cuts = pieces_of(rows)
    half = rows // 2

    def head_part(by, at, size):
        return jnp.dot(sl_ref[at : at + size, :], hn_ref[(x + by) % RING], preferred_element_type=F32)

    def x_send(slot, by, h, into, to, base, far=None):
        copies = []
        for n in range(2):
            at, size = cuts[2 * h + n]
            value = head_part(by, at, size)
            spot = pl.ds(at - h * half, size)
            if far is not None:
                value = value + x_far[far, spot, :].astype(F32)
            x_out[slot, spot, :] = value.astype(BF16)
            copies.append(link(base + n, x_out.at[slot, spot], into.at[spot], x_peer(to)))
            copies[-1].start()
        return copies

    far_r = x_send(0, 2, 0, x_far.at[0], 1, 0)
    far_l = x_send(1, 2, 1, x_far.at[1], RING - 1, 2)
    free_r = x_send(3, 1, 1, x_in.at[1], 1, 4)
    free_l = x_send(4, RING - 1, 0, x_in.at[2], RING - 1, 6)

    for at in range(0, rows, 128):
        size = min(128, rows - at)
        flat[:, at : at + size] = sl_ref[at : at + size, 0:both].T

    def term_step(i):
        w_copy(i).wait()
        value = jnp.dot(flat[:, 0:block], w_buf[i % 2], preferred_element_type=F32)
        first = w_row(i) * (chunk // sub)
        flipped = value.T
        for n in range(chunk // sub):
            terms[first + n] = flipped[n * sub : (n + 1) * sub, :]
        if i + 2 < count:
            w_copy(i + 2).start()

    pair_of = RING // 2
    p_at, q_at = pl.ds(0, tokens), pl.ds(tokens, tokens)

    def p_term(by, n):
        return terms[((z + by) % RING) * RING + n, :, p_at]

    def q_term(by, n):
        return terms[n * RING + (y + by) % RING, :, q_at]

    def ring_sum(part, out, far, into, peer, base):
        def put(slot, by, h, extra=None):
            for n, value in enumerate(part(by, h)):
                if extra is not None:
                    value = value + extra[n].astype(F32)
                out[slot, n] = value.astype(BF16)

        def start(n, slot, dst, by):
            copy = link(base + n, out.at[slot], dst, peer(by))
            copy.start()
            return copy

        held = {}

        def begin():
            put(0, 2, 0)
            held["a"] = start(0, 0, far.at[0], 1)
            put(1, 2, 1)
            held["b"] = start(1, 1, far.at[1], RING - 1)

        def free():
            put(3, 1, 1)
            held["c"] = start(2, 3, into.at[1], 1)
            put(4, RING - 1, 0)
            held["d"] = start(3, 4, into.at[2], RING - 1)

        def late():
            held["a"].wait()
            put(2, 1, 0, far.at[0])
            held["e"] = start(4, 2, into.at[0], 1)
            held["b"].wait()
            put(5, RING - 1, 1, far.at[1])
            held["f"] = start(5, 5, into.at[3], RING - 1)

        def end():
            for name in "cdef":
                held[name].wait()

        return begin, free, late, end

    def p_part(by, h):
        return [p_term(by, h * pair_of + n) for n in range(pair_of)]

    def q_part(by, h):
        return [q_term(by, h * pair_of + n) for n in range(pair_of)]

    p_begin, p_free, p_late, p_end = ring_sum(p_part, p_out, p_far, p_in, z_peer, 12)
    q_begin, q_free, q_late, q_end = ring_sum(q_part, q_out, q_far, q_in, y_peer, 18)
    for i in range(count):
        term_step(i)
        if i + 1 == per:
            p_begin()
        if i + 1 == 3 * per:
            p_free()
    q_begin()
    q_free()
    p_late()
    q_late()

    for copy in far_r:
        copy.wait()
    dep_r = x_send(2, 1, 0, x_in.at[0], 1, 8, far=0)
    for copy in far_l:
        copy.wait()
    dep_l = x_send(5, RING - 1, 1, x_in.at[3], RING - 1, 10, far=1)

    for at, size in cuts:
        keep = min(size, block - at)
        gw_ref[at : at + keep, :] = head_part(0, at, size)[0:keep]

    p_end()
    for n in range(RING):
        got = p_in[n // pair_of, n % pair_of].astype(F32) + p_in[2 + n // pair_of, n % pair_of].astype(F32)
        mine = z * RING + n
        terms[mine, :, p_at] = terms[mine, :, p_at] + got
    q_end()
    for n in range(RING):
        got = q_in[n // pair_of, n % pair_of].astype(F32) + q_in[2 + n // pair_of, n % pair_of].astype(F32)
        mine = n * RING + y
        terms[mine, :, q_at] = terms[mine, :, q_at] + got

    cut = sub // 2

    def p2_part(by, h):
        return [terms[z * RING + (y + by) % RING, h * cut : (h + 1) * cut, p_at]]

    def q2_part(by, h):
        return [terms[((z + by) % RING) * RING + y, h * cut : (h + 1) * cut, q_at]]

    p2 = ring_sum(p2_part, p2_out, p2_far, p2_in, y_peer, 24)
    q2 = ring_sum(q2_part, q2_out, q2_far, q2_in, z_peer, 30)
    for stage in range(4):
        p2[stage]()
        q2[stage]()
    for s, (lane, into) in enumerate(((p_at, p2_in), (q_at, q2_in))):
        for h in range(2):
            value = terms[tensor, h * cut : (h + 1) * cut, lane]
            value = value + into[h, 0].astype(F32) + into[2 + h, 0].astype(F32)
            gh_ref[s, h * cut : (h + 1) * cut, :] = value.astype(BF16)

    def add_in(at, size, h):
        to = at + h * half
        got = x_in[h, pl.ds(at, size), :].astype(F32) + x_in[2 + h, pl.ds(at, size), :].astype(F32)
        keep = min(size, block - to)
        gw_ref[to : to + keep, :] = gw_ref[to : to + keep, :] + got[0:keep]

    for h, from_left, from_right in ((0, dep_r, free_l), (1, free_r, dep_l)):
        for n in range(2):
            from_left[n].wait()
            from_right[n].wait()
            at, size = cuts[2 * h + n]
            for i in range(0, size, 16):
                add_in(at - h * half + i, 16, h)


def sums(sl, hn, w, steps, tokens, block):
    rows = sl.shape[0]
    d = w.shape[1]
    sub = d // PARTS
    both = steps * tokens
    width = CORES * sub
    half = rows // 2
    vmem = pl.BlockSpec(memory_space=pltpu.VMEM)
    ring_x = [(6, half, width), (2, half, width), (4, half, width)]
    ring_1 = [(6, 2, sub, tokens), (2, 2, sub, tokens), (4, 2, sub, tokens)]
    ring_2 = [(6, 1, sub // 2, tokens), (2, 1, sub // 2, tokens), (4, 1, sub // 2, tokens)]
    return pl.pallas_call(
        functools.partial(sums_kernel, (steps, tokens, block)),
        out_shape=(
            jax.ShapeDtypeStruct((steps, sub, tokens), BF16),
            jax.ShapeDtypeStruct((block, width), F32),
        ),
        in_specs=[vmem, vmem, pl.BlockSpec(memory_space=pl.ANY)],
        out_specs=(vmem, vmem),
        scratch_shapes=[
            pltpu.VMEM((both, ceil_to(rows, 128)), BF16),
            pltpu.VMEM((2, block, 2 * sub), BF16),
            pltpu.VMEM((PARTS, sub, both), F32),
        ]
        + [pltpu.VMEM(shape, BF16) for shape in ring_x + ring_1 + ring_1 + ring_2 + ring_2]
        + [
            pltpu.SemaphoreType.DMA((2,)),
            pltpu.SemaphoreType.DMA((36,)),
            pltpu.SemaphoreType.DMA((36,)),
        ],
        compiler_params=pltpu.CompilerParams(
            collective_id=3, has_side_effects=True, vmem_limit_bytes=62 * 2**20
        ),
        name="sums",
    )(sl, hn, w)


def per_device(hidden, draft_head, target_logits, draft_to_target):
    steps, tokens, _ = hidden.shape
    block = draft_to_target.shape[0] // PARTS
    heavy = block // 8
    bound = heavy + (block - heavy + PARTS - 1) // PARTS
    slots = ceil_to(bound, 16)
    w = draft_head.T
    sl, hn = front(hidden.transpose(0, 2, 1), draft_to_target.reshape(PARTS, block), target_logits.T, w, slots)
    gh, gw = sums(sl, hn, w, steps, tokens, block)
    return gh.transpose(0, 2, 1), gw.T


def solution(mesh):
    in_specs = (P(None, "dp", "tensor"), P(None, "tensor"), P("dp", "tensor"), P())
    out_specs = (P(None, "dp", "tensor"), P("dp", "tensor"))
    return jax.shard_map(
        per_device, mesh=mesh, in_specs=in_specs, out_specs=out_specs, check_vma=False
    )
```

```python
import functools

import jax
import jax.numpy as jnp
from jax import lax
from jax.experimental import pallas as pl
from jax.experimental.pallas import tpu as pltpu
from jax.sharding import PartitionSpec as P

LOSS_SCALE = 256.0
STEP_DECAY = 0.8
MESH = pl.DeviceIdType.MESH
F32 = jnp.float32
BF16 = jnp.bfloat16
I32 = jnp.int32
RING = 4
CORES = 2
PARTS = RING * RING
LOW = -3.0e38
NT = (((1,), (1,)), ((), ()))


def ceil_to(value, unit):
    return (value + unit - 1) // unit * unit


def places():
    dp = lax.axis_index("dp")
    tensor = lax.axis_index("tensor")
    x, core = dp // CORES, dp % CORES
    z, y = tensor // RING, tensor % RING
    return dp, tensor, x, core, z, y


def sweep(first, last, size, step, carry):
    full = (last - first) // size

    def go(i, value):
        return step(pl.multiple_of(first + i * size, 16), size, value)

    carry = lax.fori_loop(0, full, go, carry)
    if first + full * size < last:
        carry = step(first + full * size, last - first - full * size, carry)
    return carry


def remote(src, dst, send, recv, device):
    return pltpu.make_async_remote_copy(
        src_ref=src, dst_ref=dst, send_sem=send, recv_sem=recv, device_id=device, device_id_type=MESH
    )


def pieces_of(rows):
    half = rows // 2
    first = ceil_to(half // 2, 16)
    return [(0, first), (first, half - first), (half, first), (half + first, half - first)]


def front_kernel(
    sizes,
    hid_ref,
    ids_ref,
    logits_ref,
    w_ref,
    sl_ref,
    hn_ref,
    ht,
    h_peer,
    w_buf,
    source,
    picked,
    outgoing,
    incoming,
    expo,
    probs,
    rank_v,
    tab_v,
    place_v,
    ex1,
    ex2,
    tab_s,
    place_s,
    ag_send,
    ag_recv,
    a2a_send,
    a2a_recv,
    ex_send,
    ex_recv,
    pair_send,
    pair_recv,
    w_sem,
    s_sem,
):
    steps, tokens, block, rows, slots = sizes
    shard = logits_ref.shape[0]
    sub = hid_ref.shape[1]
    both = steps * tokens
    wide = ceil_to(block, 256)
    lane_parts = tokens // 128
    dp, tensor, x, core, z, y = places()
    partner = (x * CORES + 1 - core, tensor)

    def z_peer(by):
        return (dp, ((z + by) % RING) * RING + y)

    def y_peer(by):
        return (dp, z * RING + (y + by) % RING)

    def group_peer(i):
        return (dp, (tensor + i) % PARTS)

    chunk = w_buf.shape[2]

    def w_copy(i):
        return pltpu.make_async_copy(w_ref.at[:, pl.ds(i * chunk, chunk)], w_buf.at[i % 2], w_sem.at[i % 2])

    w_copy(0).start()
    w_copy(1).start()
    for s in range(steps):
        ht[s, z, y] = hid_ref[s]

    barrier = pltpu.get_barrier_semaphore()
    for i in range(1, PARTS):
        pl.semaphore_signal(barrier, inc=1, device_id=group_peer(i), device_id_type=MESH)
    pl.semaphore_signal(barrier, inc=1, device_id=partner, device_id_type=MESH)
    pl.semaphore_wait(barrier, PARTS)

    def gather_ring(half, at, peer, base):
        right, left = (at + 1) % RING, (at + RING - 1) % RING

        def copy(n, r, h, by):
            ref = half(r, h)
            return remote(ref, ref, ag_send.at[base + n], ag_recv.at[base + n], peer(by))

        r1 = copy(0, at, 0, 1)
        l1 = copy(1, at, 1, RING - 1)
        r2 = copy(2, at, 1, 1)
        l2 = copy(3, at, 0, RING - 1)
        for c in (r1, l1, r2, l2):
            c.start()

        def pass_on():
            r1.wait()
            r3 = copy(4, left, 0, 1)
            r3.start()
            l1.wait()
            l3 = copy(5, right, 1, RING - 1)
            l3.start()

            def finish():
                for c in (r2, l2, r3, l3):
                    c.wait()

            return finish

        return pass_on

    def half_rows(s, at_z, at_y, h):
        return ht.at[s, at_z, at_y, pl.ds(h * (sub // 2), sub // 2)]

    two = RING // 2
    p1 = gather_ring(lambda r, h: half_rows(0, z, r, h), y, y_peer, 0)
    q1 = gather_ring(lambda r, h: half_rows(1, r, y, h), z, z_peer, 6)

    def top_rows(at, size, best):
        part = logits_ref[pl.ds(at, size), :].astype(F32)
        return jnp.maximum(best, jnp.max(part.reshape(size // 8, 8, tokens), axis=0))

    best = sweep(0, shard, 64, top_rows, jnp.full((8, tokens), LOW, F32))
    peak_here = jnp.max(best, axis=0, keepdims=True)

    def exp_rows(at, size, acc):
        part = jnp.exp(logits_ref[pl.ds(at, size), :].astype(F32) - peak_here)
        for c in range(lane_parts):
            source[c, pl.ds(at, size), :] = part[:, c * 128 : (c + 1) * 128]
        return acc + jnp.sum(part.reshape(size // 8, 8, tokens), axis=0)

    acc = sweep(0, shard, 64, exp_rows, jnp.zeros((8, tokens), F32))
    total_here = jnp.sum(acc, axis=0, keepdims=True)
    row8 = lax.broadcasted_iota(I32, (8, tokens), 0)
    ex1[tensor] = jnp.where(row8 == 0, peak_here, jnp.where(row8 == 1, total_here, 0.0))
    first = [
        remote(ex1.at[tensor], ex1.at[tensor], ex_send.at[0, i], ex_recv.at[0, i], group_peer(i))
        for i in range(1, PARTS)
    ]
    for copy in first:
        copy.start()

    ids = jnp.concatenate([ids_ref[...], jnp.full((PARTS, wide - block), -1, I32)], axis=1)
    local = ids - tensor * shard
    mine = (local >= 0) & (local < shard)
    own = jnp.sum(jnp.where(lax.broadcasted_iota(I32, (PARTS, wide), 0) == tensor, ids, 0), axis=0, keepdims=True)
    start = lax.broadcasted_iota(I32, (PARTS, wide), 0) * shard
    from_owner = (own >= start) & (own < start + shard)
    hits = jnp.concatenate([jnp.where(mine, 1.0, 0.0), jnp.where(from_owner, 1.0, 0.0)], axis=0)
    before = lax.broadcasted_iota(I32, (256, 256), 0)
    after = lax.broadcasted_iota(I32, (256, 256), 1)
    upper = jnp.where(before <= after, 1.0, 0.0).astype(BF16)
    seen = jnp.full((2 * PARTS, 1), -1.0, F32)
    rank_list = []
    for n in range(wide // 256):
        part = hits[:, n * 256 : (n + 1) * 256]
        rank_list.append(jnp.dot(part.astype(BF16), upper, preferred_element_type=F32) + seen)
        seen = seen + jnp.sum(part, axis=1, keepdims=True)
    ranks = jnp.concatenate(rank_list, axis=1)
    owner = lax.broadcasted_iota(I32, (PARTS, wide), 0).astype(F32) * float(slots)
    place = jnp.sum(jnp.where(from_owner, owner + ranks[PARTS:], 0.0), axis=0, keepdims=True)
    place_v[...] = jnp.clip(jnp.broadcast_to(place, (8, wide)).astype(I32), 0, PARTS * slots - 1)
    rank_v[0] = jnp.where(mine, ranks[:PARTS], -1.0)
    rank_v[1] = jnp.where(mine, local - (local & 255), 0).astype(F32)
    rank_v[2] = jnp.where(mine, local & 255, 0).astype(F32)
    to_place = pltpu.make_async_copy(place_v, place_s, s_sem.at[0])
    to_place.start()

    p1_end = p1()
    q1_end = q1()

    slot = lax.broadcasted_iota(I32, (tab_v.shape[1], wide), 0).astype(F32)
    kind = lax.broadcasted_iota(I32, (8, wide), 0)

    def table_step(b, _):
        rank = rank_v[0, pl.ds(b, 1), :]
        info = jnp.where(kind == 0, rank_v[1, pl.ds(b, 1), :], jnp.where(kind == 1, rank_v[2, pl.ds(b, 1), :], 0.0))
        hot = jnp.where(slot == rank, 1.0, 0.0).astype(BF16)
        got = lax.dot_general(info.astype(BF16), hot, NT, preferred_element_type=F32)
        found = (got[0:1, :] + got[1:2, :]).astype(I32)
        tab_v[pl.ds(b, 1), :] = jnp.clip(found, 0, shard - 1)
        return 0

    lax.fori_loop(0, two, table_step, 0)
    p1_end()
    q1_end()
    p2 = gather_ring(lambda r, h: ht.at[0, r, pl.ds(h * two, two)], z, z_peer, 12)
    q2 = gather_ring(lambda r, h: ht.at[1, pl.ds(h * two, two), r], y, y_peer, 18)
    lax.fori_loop(two, PARTS, table_step, 0)
    to_tab = pltpu.make_async_copy(tab_v, tab_s, s_sem.at[1])
    to_tab.start()

    for copy in first:
        copy.wait()
    peaks = [ex1[i, 0:1, :] for i in range(PARTS)]
    peak = functools.reduce(jnp.maximum, peaks)
    total = sum(ex1[i, 1:2, :] * jnp.exp(peaks[i] - peak) for i in range(PARTS))
    share = jnp.exp(peak_here - peak) / total
    to_tab.wait()
    to_place.wait()

    def pick(index_of, count):
        def go(i, _):
            got = []
            for r in range(16):
                at = index_of(i * 16 + r)
                got.append([source[c, pl.ds(at, 1), :] for c in range(lane_parts)])
            for r in range(16):
                for c in range(lane_parts):
                    picked[c, pl.ds(i * 16 + r, 1), :] = got[r][c]
            return 0

        lax.fori_loop(0, count // 16, go, 0)

    def joined(at, size):
        return jnp.concatenate([picked[c, pl.ds(at, size), :] for c in range(lane_parts)], axis=1)

    def sent(i):
        to = (tensor + i) % PARTS
        return remote(outgoing.at[to], incoming.at[tensor], a2a_send.at[i], a2a_recv.at[i], (dp, to))

    def send_step(i, _):
        to = (tensor + i) % PARTS
        pick(lambda j: tab_s[to, j], slots)
        outgoing[to] = (joined(0, slots) * share).astype(BF16)
        sent(i).start()
        return 0

    lax.fori_loop(1, two * RING, send_step, 0)
    p2_end = p2()
    q2_end = q2()
    lax.fori_loop(two * RING, PARTS, send_step, 0)
    pick(lambda j: tab_s[tensor, j], slots)
    incoming[tensor] = (joined(0, slots) * share).astype(BF16)

    p2_end()
    q2_end()
    swap_h = remote(
        ht.at[:, :, pl.ds((1 - core) * CORES, CORES)], h_peer, pair_send.at[0], pair_recv.at[0], partner
    )
    swap_h.start()

    pieces = PARTS * sub // chunk
    each = chunk // sub
    expo[...] = jnp.zeros((rows, both), F32)

    def score_step(i, _):
        w_copy(i).wait()
        for s in range(steps):
            at = i * each
            h = ht[s, at // RING, pl.ds(at % RING, each)].reshape(chunk, tokens)
            lanes = slice(s * tokens, (s + 1) * tokens)
            expo[0:block, lanes] += jnp.dot(w_buf[i % 2], h, preferred_element_type=F32)

        @pl.when(i + 2 < pieces)
        def _():
            w_copy(i + 2).start()

        return 0

    lax.fori_loop(0, pieces, score_step, 0)
    if rows > block:
        expo[block:rows, :] = jnp.full((rows - block, both), LOW, F32)

    def top_step(at, size, m):
        return jnp.maximum(m, jnp.max(expo[pl.ds(at, size), :].reshape(size // 8, 8, both), axis=0))

    top = sweep(0, rows, 32, top_step, jnp.full((8, both), LOW, F32))
    top = jnp.max(top, axis=0, keepdims=True)

    def exp_step(at, size, a):
        value = jnp.exp(expo[pl.ds(at, size), :] - top)
        expo[pl.ds(at, size), :] = value
        return a + jnp.sum(value.reshape(size // 8, 8, both), axis=0)

    weight = sweep(0, rows, 32, exp_step, jnp.zeros((8, both), F32))
    weight = jnp.sum(weight, axis=0, keepdims=True)

    own_rows = CORES * sub
    for i in range(RING):
        for s in range(steps):
            part = ht[s, i, pl.ds(core * CORES, CORES)].reshape(own_rows, tokens)
            hn_ref[i, s * tokens : (s + 1) * tokens, :] = part.T
    swap_h.wait()
    for i in range(RING):
        for s in range(steps):
            part = h_peer[s, i].reshape(own_rows, tokens)
            hn_ref[i, both + s * tokens : both + (s + 1) * tokens, :] = part.T

    def widen_in(i):
        part = incoming[i].astype(F32)
        for c in range(lane_parts):
            source[c, pl.ds(pl.multiple_of(i * slots, 16), slots), :] = part[:, c * 128 : (c + 1) * 128]

    widen_in(tensor)

    def arrived(i, _):
        sent(i).wait()
        widen_in((tensor + PARTS - i) % PARTS)
        return 0

    lax.fori_loop(1, PARTS, arrived, 0)
    pick(lambda j: place_s[0, j], rows)
    if rows > block:
        for c in range(lane_parts):
            picked[c, block:rows, :] = jnp.zeros((rows - block, 128), F32)

    def mass_step(at, size, a):
        return a + jnp.sum(joined(at, size).reshape(size // 8, 8, tokens), axis=0)

    mass_here = sweep(0, rows, 96, mass_step, jnp.zeros((8, tokens), F32))
    mass_here = jnp.sum(mass_here, axis=0, keepdims=True)

    row8 = lax.broadcasted_iota(I32, (8, both), 0)
    mass_wide = jnp.concatenate([mass_here] * steps, axis=1)
    ex2[tensor] = jnp.where(row8 == 0, top, jnp.where(row8 == 1, weight, jnp.where(row8 == 2, mass_wide, 0.0)))
    second = [
        remote(ex2.at[tensor], ex2.at[tensor], ex_send.at[1, i], ex_recv.at[1, i], group_peer(i))
        for i in range(1, PARTS)
    ]
    for copy in second:
        copy.start()

    scales = [LOSS_SCALE * STEP_DECAY**s for s in range(steps)]

    def shift(value, step):
        if step == 0:
            return value
        lane = lax.broadcasted_iota(I32, value.shape, 1)
        return jnp.where(lane < tokens - step, pltpu.roll(value, tokens - step, 1), 0.0)

    def shift_step(at, size, _):
        value = joined(at, size)
        for s in range(steps):
            probs[s, pl.ds(at, size), :] = scales[s] * shift(value, s)
        return 0

    sweep(0, rows, 96, shift_step, 0)
    for copy in second:
        copy.wait()
    tops = [ex2[i, 0:1, :] for i in range(PARTS)]
    top_all = functools.reduce(jnp.maximum, tops)
    weight_all = sum(ex2[i, 1:2, :] * jnp.exp(tops[i] - top_all) for i in range(PARTS))
    mass = sum(ex2[i, 2:3, 0:tokens] for i in range(PARTS))

    factor = jnp.exp(top - top_all) / weight_all
    coefs = []
    for s in range(steps):
        moved = shift(jnp.broadcast_to(mass, (8, tokens)), s)[0:1, :]
        coefs.append(scales[s] * moved * factor[:, s * tokens : (s + 1) * tokens])

    def slope_step(at, size, _):
        for s in range(steps):
            lanes = slice(s * tokens, (s + 1) * tokens)
            value = expo[pl.ds(at, size), lanes] * coefs[s] - probs[s, pl.ds(at, size), :]
            sl_ref[pl.ds(at, size), lanes] = value.astype(BF16)
        return 0

    swaps = []
    for n, (at, size) in enumerate(pieces_of(rows)):
        sweep(at, at + size, 96, slope_step, 0)
        swaps.append(
            remote(
                sl_ref.at[pl.ds(at, size), pl.ds(0, both)],
                sl_ref.at[pl.ds(at, size), pl.ds(both, both)],
                pair_send.at[1 + n],
                pair_recv.at[1 + n],
                partner,
            )
        )
        swaps[-1].start()
    for copy in swaps:
        copy.wait()


def front(hid, ids, logits, w, slots):
    steps, sub, tokens = hid.shape
    parts, block = ids.shape
    shard = logits.shape[0]
    both = steps * tokens
    rows = ceil_to(block, 32)
    wide = ceil_to(block, 256)
    depth = ceil_to(max(shard, parts * slots), 32)
    vmem = pl.BlockSpec(memory_space=pltpu.VMEM)
    return pl.pallas_call(
        functools.partial(front_kernel, (steps, tokens, block, rows, slots)),
        out_shape=(
            jax.ShapeDtypeStruct((rows, CORES * both), BF16),
            jax.ShapeDtypeStruct((RING, CORES * both, CORES * sub), BF16),
        ),
        in_specs=[vmem, vmem, vmem, pl.BlockSpec(memory_space=pl.ANY)],
        out_specs=(vmem, vmem),
        scratch_shapes=[
            pltpu.VMEM((steps, RING, RING, sub, tokens), BF16),
            pltpu.VMEM((steps, RING, CORES, sub, tokens), BF16),
            pltpu.VMEM((2, block, 2 * sub), BF16),
            pltpu.VMEM((tokens // 128, depth, 128), F32),
            pltpu.VMEM((tokens // 128, ceil_to(max(rows, slots), 16), 128), F32),
            pltpu.VMEM((parts, slots, tokens), BF16),
            pltpu.VMEM((parts, slots, tokens), BF16),
            pltpu.VMEM((rows, both), F32),
            pltpu.VMEM((steps, rows, tokens), F32),
            pltpu.VMEM((3, parts, wide), F32),
            pltpu.VMEM((parts, ceil_to(slots, 128)), I32),
            pltpu.VMEM((8, wide), I32),
            pltpu.VMEM((parts, 8, tokens), F32),
            pltpu.VMEM((parts, 8, both), F32),
            pltpu.SMEM((parts, ceil_to(slots, 128)), I32),
            pltpu.SMEM((8, wide), I32),
            pltpu.SemaphoreType.DMA((24,)),
            pltpu.SemaphoreType.DMA((24,)),
            pltpu.SemaphoreType.DMA((parts,)),
            pltpu.SemaphoreType.DMA((parts,)),
            pltpu.SemaphoreType.DMA((2, parts)),
            pltpu.SemaphoreType.DMA((2, parts)),
            pltpu.SemaphoreType.DMA((5,)),
            pltpu.SemaphoreType.DMA((5,)),
            pltpu.SemaphoreType.DMA((2,)),
            pltpu.SemaphoreType.DMA((2,)),
        ],
        compiler_params=pltpu.CompilerParams(
            collective_id=2, has_side_effects=True, vmem_limit_bytes=62 * 2**20
        ),
        name="front",
    )(hid, ids, logits, w)


def sums_kernel(
    sizes,
    sl_ref,
    hn_ref,
    w_ref,
    gh_ref,
    gw_ref,
    flat,
    w_buf,
    terms,
    x_out,
    x_far,
    x_in,
    p_out,
    p_far,
    p_in,
    q_out,
    q_far,
    q_in,
    p2_out,
    p2_far,
    p2_in,
    q2_out,
    q2_far,
    q2_in,
    w_sem,
    ring_send,
    ring_recv,
):
    steps, tokens, block = sizes
    rows = sl_ref.shape[0]
    both = steps * tokens
    dp, tensor, x, core, z, y = places()
    sub = gh_ref.shape[1]
    chunk = w_buf.shape[2]

    def x_peer(by):
        return (((x + by) % RING) * CORES + core, tensor)

    def z_peer(by):
        return (dp, ((z + by) % RING) * RING + y)

    def y_peer(by):
        return (dp, z * RING + (y + by) % RING)

    per = RING * sub // chunk
    count = RING * per

    def w_row(i):
        order = (2, 1, RING - 1, 0)[i // per]
        return ((z + order) % RING) * per + i % per

    def w_copy(i):
        at = pl.multiple_of(w_row(i) * chunk, chunk)
        return pltpu.make_async_copy(w_ref.at[:, pl.ds(at, chunk)], w_buf.at[i % 2], w_sem.at[i % 2])

    w_copy(0).start()
    w_copy(1).start()

    barrier = pltpu.get_barrier_semaphore()
    for peer in (x_peer, y_peer, z_peer):
        for by in (1, RING - 1):
            pl.semaphore_signal(barrier, inc=1, device_id=peer(by), device_id_type=MESH)
    pl.semaphore_wait(barrier, 6)

    def link(n, src, dst, device):
        return remote(src, dst, ring_send.at[n], ring_recv.at[n], device)

    cuts = pieces_of(rows)
    half = rows // 2

    def head_part(by, at, size):
        return jnp.dot(sl_ref[at : at + size, :], hn_ref[(x + by) % RING], preferred_element_type=F32)

    def x_send(slot, by, h, into, to, base, far=None):
        copies = []
        for n in range(2):
            at, size = cuts[2 * h + n]
            value = head_part(by, at, size)
            spot = pl.ds(at - h * half, size)
            if far is not None:
                value = value + x_far[far, spot, :].astype(F32)
            x_out[slot, spot, :] = value.astype(BF16)
            copies.append(link(base + n, x_out.at[slot, spot], into.at[spot], x_peer(to)))
            copies[-1].start()
        return copies

    far_r = x_send(0, 2, 0, x_far.at[0], 1, 0)
    far_l = x_send(1, 2, 1, x_far.at[1], RING - 1, 2)
    free_r = x_send(3, 1, 1, x_in.at[1], 1, 4)
    free_l = x_send(4, RING - 1, 0, x_in.at[2], RING - 1, 6)

    for at in range(0, rows, 128):
        size = min(128, rows - at)
        flat[:, at : at + size] = sl_ref[at : at + size, 0:both].T

    def term_step(i):
        w_copy(i).wait()
        value = jnp.dot(flat[:, 0:block], w_buf[i % 2], preferred_element_type=F32)
        first = w_row(i) * (chunk // sub)
        flipped = value.T
        for n in range(chunk // sub):
            terms[first + n] = flipped[n * sub : (n + 1) * sub, :]
        if i + 2 < count:
            w_copy(i + 2).start()

    pair_of = RING // 2
    p_at, q_at = pl.ds(0, tokens), pl.ds(tokens, tokens)

    def p_term(by, n):
        return terms[((z + by) % RING) * RING + n, :, p_at]

    def q_term(by, n):
        return terms[n * RING + (y + by) % RING, :, q_at]

    def ring_sum(part, out, far, into, peer, base):
        def put(slot, by, h, extra=None):
            for n, value in enumerate(part(by, h)):
                if extra is not None:
                    value = value + extra[n].astype(F32)
                out[slot, n] = value.astype(BF16)

        def start(n, slot, dst, by):
            copy = link(base + n, out.at[slot], dst, peer(by))
            copy.start()
            return copy

        held = {}

        def begin():
            put(0, 2, 0)
            held["a"] = start(0, 0, far.at[0], 1)
            put(1, 2, 1)
            held["b"] = start(1, 1, far.at[1], RING - 1)

        def free():
            put(3, 1, 1)
            held["c"] = start(2, 3, into.at[1], 1)
            put(4, RING - 1, 0)
            held["d"] = start(3, 4, into.at[2], RING - 1)

        def late():
            held["a"].wait()
            put(2, 1, 0, far.at[0])
            held["e"] = start(4, 2, into.at[0], 1)
            held["b"].wait()
            put(5, RING - 1, 1, far.at[1])
            held["f"] = start(5, 5, into.at[3], RING - 1)

        def end():
            for name in "cdef":
                held[name].wait()

        return begin, free, late, end

    def p_part(by, h):
        return [p_term(by, h * pair_of + n) for n in range(pair_of)]

    def q_part(by, h):
        return [q_term(by, h * pair_of + n) for n in range(pair_of)]

    p_begin, p_free, p_late, p_end = ring_sum(p_part, p_out, p_far, p_in, z_peer, 12)
    q_begin, q_free, q_late, q_end = ring_sum(q_part, q_out, q_far, q_in, y_peer, 18)
    for i in range(count):
        term_step(i)
        if i + 1 == per:
            p_begin()
        if i + 1 == 3 * per:
            p_free()
    q_begin()
    q_free()
    p_late()
    q_late()

    for copy in far_r:
        copy.wait()
    dep_r = x_send(2, 1, 0, x_in.at[0], 1, 8, far=0)
    for copy in far_l:
        copy.wait()
    dep_l = x_send(5, RING - 1, 1, x_in.at[3], RING - 1, 10, far=1)

    for at, size in cuts:
        keep = min(size, block - at)
        gw_ref[at : at + keep, :] = head_part(0, at, size)[0:keep]

    p_end()
    for n in range(RING):
        got = p_in[n // pair_of, n % pair_of].astype(F32) + p_in[2 + n // pair_of, n % pair_of].astype(F32)
        mine = z * RING + n
        terms[mine, :, p_at] = terms[mine, :, p_at] + got
    q_end()
    for n in range(RING):
        got = q_in[n // pair_of, n % pair_of].astype(F32) + q_in[2 + n // pair_of, n % pair_of].astype(F32)
        mine = n * RING + y
        terms[mine, :, q_at] = terms[mine, :, q_at] + got

    cut = sub // 2

    def p2_part(by, h):
        return [terms[z * RING + (y + by) % RING, h * cut : (h + 1) * cut, p_at]]

    def q2_part(by, h):
        return [terms[((z + by) % RING) * RING + y, h * cut : (h + 1) * cut, q_at]]

    p2 = ring_sum(p2_part, p2_out, p2_far, p2_in, y_peer, 24)
    q2 = ring_sum(q2_part, q2_out, q2_far, q2_in, z_peer, 30)
    for stage in range(4):
        p2[stage]()
        q2[stage]()
    for s, (lane, into) in enumerate(((p_at, p2_in), (q_at, q2_in))):
        for h in range(2):
            value = terms[tensor, h * cut : (h + 1) * cut, lane]
            value = value + into[h, 0].astype(F32) + into[2 + h, 0].astype(F32)
            gh_ref[s, h * cut : (h + 1) * cut, :] = value.astype(BF16)

    def add_in(at, size, h):
        to = at + h * half
        got = x_in[h, pl.ds(at, size), :].astype(F32) + x_in[2 + h, pl.ds(at, size), :].astype(F32)
        keep = min(size, block - to)
        gw_ref[to : to + keep, :] = gw_ref[to : to + keep, :] + got[0:keep]

    for h, from_left, from_right in ((0, dep_r, free_l), (1, free_r, dep_l)):
        for n in range(2):
            from_left[n].wait()
            from_right[n].wait()
            at, size = cuts[2 * h + n]
            for i in range(0, size, 16):
                add_in(at - h * half + i, 16, h)


def sums(sl, hn, w, steps, tokens, block):
    rows = sl.shape[0]
    d = w.shape[1]
    sub = d // PARTS
    both = steps * tokens
    width = CORES * sub
    half = rows // 2
    vmem = pl.BlockSpec(memory_space=pltpu.VMEM)
    ring_x = [(6, half, width), (2, half, width), (4, half, width)]
    ring_1 = [(6, 2, sub, tokens), (2, 2, sub, tokens), (4, 2, sub, tokens)]
    ring_2 = [(6, 1, sub // 2, tokens), (2, 1, sub // 2, tokens), (4, 1, sub // 2, tokens)]
    return pl.pallas_call(
        functools.partial(sums_kernel, (steps, tokens, block)),
        out_shape=(
            jax.ShapeDtypeStruct((steps, sub, tokens), BF16),
            jax.ShapeDtypeStruct((block, width), F32),
        ),
        in_specs=[vmem, vmem, pl.BlockSpec(memory_space=pl.ANY)],
        out_specs=(vmem, vmem),
        scratch_shapes=[
            pltpu.VMEM((both, ceil_to(rows, 128)), BF16),
            pltpu.VMEM((2, block, 2 * sub), BF16),
            pltpu.VMEM((PARTS, sub, both), F32),
        ]
        + [pltpu.VMEM(shape, BF16) for shape in ring_x + ring_1 + ring_1 + ring_2 + ring_2]
        + [
            pltpu.SemaphoreType.DMA((2,)),
            pltpu.SemaphoreType.DMA((36,)),
            pltpu.SemaphoreType.DMA((36,)),
        ],
        compiler_params=pltpu.CompilerParams(
            collective_id=3, has_side_effects=True, vmem_limit_bytes=62 * 2**20
        ),
        name="sums",
    )(sl, hn, w)


def per_device(hidden, draft_head, target_logits, draft_to_target):
    steps, tokens, _ = hidden.shape
    block = draft_to_target.shape[0] // PARTS
    heavy = block // 8
    bound = heavy + (block - heavy + PARTS - 1) // PARTS
    slots = ceil_to(bound, 16)
    w = draft_head.T
    sl, hn = front(hidden.transpose(0, 2, 1), draft_to_target.reshape(PARTS, block), target_logits.T, w, slots)
    gh, gw = sums(sl, hn, w, steps, tokens, block)
    return gh.transpose(0, 2, 1), gw.T


def solution(mesh):
    in_specs = (P(None, "dp", "tensor"), P(None, "tensor"), P("dp", "tensor"), P())
    out_specs = (P(None, "dp", "tensor"), P("dp", "tensor"))
    return jax.shard_map(
        per_device, mesh=mesh, in_specs=in_specs, out_specs=out_specs, check_vma=False
    )
```

```python
import functools

import jax
import jax.numpy as jnp
from jax import lax
from jax.experimental import pallas as pl
from jax.experimental.pallas import tpu as pltpu
from jax.sharding import PartitionSpec as P

LOSS_SCALE = 256.0
STEP_DECAY = 0.8
MESH = pl.DeviceIdType.MESH
F32 = jnp.float32
BF16 = jnp.bfloat16
I32 = jnp.int32
RING = 4
CORES = 2
PARTS = RING * RING
LOW = -3.0e38
HELD = 4
NT = (((1,), (1,)), ((), ()))


def ceil_to(value, unit):
    return (value + unit - 1) // unit * unit


def places():
    dp = lax.axis_index("dp")
    tensor = lax.axis_index("tensor")
    x, core = dp // CORES, dp % CORES
    z, y = tensor // RING, tensor % RING
    return dp, tensor, x, core, z, y


def sweep(first, last, size, step, carry):
    full = (last - first) // size

    def go(i, value):
        return step(pl.multiple_of(first + i * size, 16), size, value)

    carry = lax.fori_loop(0, full, go, carry)
    if first + full * size < last:
        carry = step(first + full * size, last - first - full * size, carry)
    return carry


def remote(src, dst, send, recv, device):
    return pltpu.make_async_remote_copy(
        src_ref=src, dst_ref=dst, send_sem=send, recv_sem=recv, device_id=device, device_id_type=MESH
    )


def pieces_of(rows):
    half = rows // 2
    first = ceil_to(half // 2, 16)
    return [(0, first), (first, half - first), (half, first), (half + first, half - first)]


def kernel(
    sizes,
    hid_ref,
    ids_ref,
    logits_hbm,
    w_ref,
    gh_ref,
    gw_ref,
    tiles,
    arena,
    floats,
    hn,
    sl,
    w_buf,
    picked,
    expo,
    moved,
    flat,
    rank_v,
    tab_v,
    place_v,
    ex1,
    ex2,
    x_out,
    x_far,
    x_in,
    tab_s,
    place_s,
    ag_send,
    ag_recv,
    a2a_send,
    a2a_recv,
    ex_send,
    ex_recv,
    pair_send,
    pair_recv,
    w_sem,
    s_sem,
    ring_send,
    ring_recv,
):
    logits_in = pltpu.make_async_copy(logits_hbm, arena, s_sem.at[2])
    logits_in.start()
    steps, tokens, block, rows, slots = sizes
    shard = arena.shape[0]
    sub = hid_ref.shape[1]
    both = steps * tokens
    wide = ceil_to(block, 256)
    lane_parts = tokens // 128
    dp, tensor, x, core, z, y = places()
    partner = (x * CORES + 1 - core, tensor)

    def x_peer(by):
        return (((x + by) % RING) * CORES + core, tensor)

    def z_peer(by):
        return (dp, ((z + by) % RING) * RING + y)

    def y_peer(by):
        return (dp, z * RING + (y + by) % RING)

    def group_peer(i):
        return (dp, (tensor + i) % PARTS)

    chunk = w_buf.shape[2]

    def w_copy(i):
        return pltpu.make_async_copy(w_ref.at[:, pl.ds(i * chunk, chunk)], w_buf.at[i % 2], w_sem.at[i % 2])

    w_copy(0).start()
    w_copy(1).start()
    for s in range(steps):
        tiles[s, z, y] = hid_ref[s]

    barrier = pltpu.get_barrier_semaphore()
    for i in range(1, PARTS):
        pl.semaphore_signal(barrier, inc=1, device_id=group_peer(i), device_id_type=MESH)
    pl.semaphore_signal(barrier, inc=1, device_id=partner, device_id_type=MESH)
    for by in (1, RING - 1):
        pl.semaphore_signal(barrier, inc=1, device_id=x_peer(by), device_id_type=MESH)
    pl.semaphore_wait(barrier, PARTS + 2)

    def gather_ring(half, at, peer, base):
        right, left = (at + 1) % RING, (at + RING - 1) % RING

        def copy(n, r, h, by):
            ref = half(r, h)
            return remote(ref, ref, ag_send.at[base + n], ag_recv.at[base + n], peer(by))

        r1 = copy(0, at, 0, 1)
        l1 = copy(1, at, 1, RING - 1)
        r2 = copy(2, at, 1, 1)
        l2 = copy(3, at, 0, RING - 1)
        for c in (r1, l1, r2, l2):
            c.start()

        def pass_on():
            r1.wait()
            r3 = copy(4, left, 0, 1)
            r3.start()
            l1.wait()
            l3 = copy(5, right, 1, RING - 1)
            l3.start()

            def finish():
                for c in (r2, l2, r3, l3):
                    c.wait()

            return finish

        return pass_on

    def half_rows(s, at_z, at_y, h):
        return tiles.at[s, at_z, at_y, pl.ds(h * (sub // 2), sub // 2)]

    two = RING // 2
    p1 = gather_ring(lambda r, h: half_rows(0, z, r, h), y, y_peer, 0)
    q1 = gather_ring(lambda r, h: half_rows(1, r, y, h), z, z_peer, 6)

    def top_rows(at, size, best):
        part = arena[pl.ds(at, size), :].astype(F32)
        return jnp.maximum(best, jnp.max(part.reshape(size // 8, 8, tokens), axis=0))

    logits_in.wait()
    best = sweep(0, shard, 64, top_rows, jnp.full((8, tokens), LOW, F32))
    peak_here = jnp.max(best, axis=0, keepdims=True)

    def exp_rows(at, size, acc):
        part = jnp.exp(arena[pl.ds(at, size), :].astype(F32) - peak_here)
        for c in range(lane_parts):
            floats[c, pl.ds(at, size), :] = part[:, c * 128 : (c + 1) * 128]
        return acc + jnp.sum(part.reshape(size // 8, 8, tokens), axis=0)

    acc = sweep(0, shard, 64, exp_rows, jnp.zeros((8, tokens), F32))
    total_here = jnp.sum(acc, axis=0, keepdims=True)
    row8 = lax.broadcasted_iota(I32, (8, tokens), 0)
    ex1[tensor] = jnp.where(row8 == 0, peak_here, jnp.where(row8 == 1, total_here, 0.0))
    first = [
        remote(ex1.at[tensor], ex1.at[tensor], ex_send.at[0, i], ex_recv.at[0, i], group_peer(i))
        for i in range(1, PARTS)
    ]
    for copy in first:
        copy.start()

    ids = jnp.concatenate([ids_ref[...], jnp.full((PARTS, wide - block), -1, I32)], axis=1)
    local = ids - tensor * shard
    mine = (local >= 0) & (local < shard)
    own = jnp.sum(jnp.where(lax.broadcasted_iota(I32, (PARTS, wide), 0) == tensor, ids, 0), axis=0, keepdims=True)
    start = lax.broadcasted_iota(I32, (PARTS, wide), 0) * shard
    from_owner = (own >= start) & (own < start + shard)
    hits = jnp.concatenate([jnp.where(mine, 1.0, 0.0), jnp.where(from_owner, 1.0, 0.0)], axis=0)
    before = lax.broadcasted_iota(I32, (256, 256), 0)
    after = lax.broadcasted_iota(I32, (256, 256), 1)
    upper = jnp.where(before <= after, 1.0, 0.0).astype(BF16)
    seen = jnp.full((2 * PARTS, 1), -1.0, F32)
    rank_list = []
    for n in range(wide // 256):
        part = hits[:, n * 256 : (n + 1) * 256]
        rank_list.append(jnp.dot(part.astype(BF16), upper, preferred_element_type=F32) + seen)
        seen = seen + jnp.sum(part, axis=1, keepdims=True)
    ranks = jnp.concatenate(rank_list, axis=1)
    owner = lax.broadcasted_iota(I32, (PARTS, wide), 0).astype(F32) * float(slots)
    place = jnp.sum(jnp.where(from_owner, owner + ranks[PARTS:], 0.0), axis=0, keepdims=True)
    place_v[...] = jnp.clip(jnp.broadcast_to(place, (8, wide)).astype(I32), 0, PARTS * slots - 1)
    rank_v[0] = jnp.where(mine, ranks[:PARTS], -1.0)
    rank_v[1] = jnp.where(mine, local - (local & 255), 0).astype(F32)
    rank_v[2] = jnp.where(mine, local & 255, 0).astype(F32)
    to_place = pltpu.make_async_copy(place_v, place_s, s_sem.at[0])
    to_place.start()

    p1_end = p1()
    q1_end = q1()

    slot = (lax.broadcasted_iota(I32, (slots // 16, 16, wide), 0) * 16).astype(F32)
    slot = slot + lax.broadcasted_iota(I32, (slots // 16, 16, wide), 1).astype(F32)
    slot = (slot - 128.0).astype(BF16)
    kind = lax.broadcasted_iota(I32, (8, wide), 0)

    tab_v[...] = jnp.zeros_like(tab_v)

    def table_step(b, _):
        rank = jnp.minimum(rank_v[0, pl.ds(b, 1), :], float(slots)) - 128.0
        rank = jnp.broadcast_to(rank, (16, wide)).astype(BF16)
        info = jnp.where(kind == 0, rank_v[1, pl.ds(b, 1), :], jnp.where(kind == 1, rank_v[2, pl.ds(b, 1), :], 0.0))
        hot = jnp.where(slot == rank[None], jnp.ones((), BF16), jnp.zeros((), BF16)).reshape(slots, wide)
        got = lax.dot_general(info.astype(BF16), hot, NT, preferred_element_type=F32)
        found = (got[0:1, :] + got[1:2, :]).astype(I32)
        tab_v[pl.ds(b, 1), 0:slots] = jnp.clip(found, 0, shard - 1)
        return 0

    lax.fori_loop(0, two, table_step, 0)
    p1_end()
    q1_end()
    p2 = gather_ring(lambda r, h: tiles.at[0, r, pl.ds(h * two, two)], z, z_peer, 12)
    q2 = gather_ring(lambda r, h: tiles.at[1, pl.ds(h * two, two), r], y, y_peer, 18)
    lax.fori_loop(two, PARTS, table_step, 0)
    to_tab = pltpu.make_async_copy(tab_v, tab_s, s_sem.at[1])
    to_tab.start()

    for copy in first:
        copy.wait()
    peaks = [ex1[i, 0:1, :] for i in range(PARTS)]
    peak = functools.reduce(jnp.maximum, peaks)
    total = sum(ex1[i, 1:2, :] * jnp.exp(peaks[i] - peak) for i in range(PARTS))
    share = jnp.exp(peak_here - peak) / total
    to_tab.wait()
    to_place.wait()

    def pick(index_of, count):
        def go(i, _):
            got = []
            for r in range(16):
                at = index_of(i * 16 + r)
                got.append([floats[c, pl.ds(at, 1), :] for c in range(lane_parts)])
            for r in range(16):
                for c in range(lane_parts):
                    picked[c, pl.ds(i * 16 + r, 1), :] = got[r][c]
            return 0

        lax.fori_loop(0, count // 16, go, 0)

    def joined(at, size):
        return jnp.concatenate([picked[c, pl.ds(at, size), :] for c in range(lane_parts)], axis=1)

    def out_at(i):
        return arena.at[pl.ds(pl.multiple_of(i * slots, 16), slots)]

    def in_at(i):
        return arena.at[pl.ds(pl.multiple_of((PARTS + i) * slots, 16), slots)]

    def sent(i):
        to = (tensor + i) % PARTS
        return remote(out_at(to), in_at(tensor), a2a_send.at[i], a2a_recv.at[i], (dp, to))

    def pick_step(i, _):
        to = (tensor + i) % PARTS
        pick(lambda j: tab_s[to, j], slots)
        out_at(to)[...] = (joined(0, slots) * share).astype(BF16)
        return 0

    def send_step(i, _):
        sent(i).start()
        return 0

    def both_step(i, _):
        pick_step(i, 0)
        return send_step(i, 0)

    lax.fori_loop(1, HELD, pick_step, 0)
    p2_end = p2()
    q2_end = q2()
    lax.fori_loop(HELD, PARTS, pick_step, 0)
    pick(lambda j: tab_s[tensor, j], slots)
    in_at(tensor)[...] = (joined(0, slots) * share).astype(BF16)

    p2_end()
    q2_end()
    lax.fori_loop(1, PARTS, send_step, 0)
    swap_h = [
        remote(
            tiles.at[s, :, pl.ds((1 - core) * CORES, CORES)],
            tiles.at[steps, :, pl.ds(s * CORES, CORES)],
            pair_send.at[4 + s],
            pair_recv.at[4 + s],
            partner,
        )
        for s in range(steps)
    ]
    for copy in swap_h:
        copy.start()

    pieces = PARTS * sub // chunk
    each = chunk // sub
    expo[...] = jnp.zeros((rows, both), F32)

    def score_step(i, _):
        w_copy(i).wait()
        for s in range(steps):
            at = i * each
            h = tiles[s, at // RING, pl.ds(at % RING, each)].reshape(chunk, tokens)
            lanes = slice(s * tokens, (s + 1) * tokens)
            expo[0:block, lanes] += jnp.dot(w_buf[i % 2], h, preferred_element_type=F32)

        @pl.when(i + 2 < pieces)
        def _():
            w_copy(i + 2).start()

        return 0

    lax.fori_loop(0, pieces, score_step, 0)

    per = RING * sub // chunk
    count = RING * per

    def w_row(i):
        order = (2, 1, RING - 1, 0)[i // per]
        return ((z + order) % RING) * per + i % per

    def w_again(i):
        at = pl.multiple_of(w_row(i) * chunk, chunk)
        return pltpu.make_async_copy(w_ref.at[:, pl.ds(at, chunk)], w_buf.at[i % 2], w_sem.at[i % 2])

    w_again(0).start()
    w_again(1).start()
    if rows > block:
        expo[block:rows, :] = jnp.full((rows - block, both), LOW, F32)

    def top_step(at, size, m):
        return jnp.maximum(m, jnp.max(expo[pl.ds(at, size), :].reshape(size // 8, 8, both), axis=0))

    top = sweep(0, rows, 32, top_step, jnp.full((8, both), LOW, F32))
    top = jnp.max(top, axis=0, keepdims=True)

    def exp_step(at, size, a):
        value = jnp.exp(expo[pl.ds(at, size), :] - top)
        expo[pl.ds(at, size), :] = value
        return a + jnp.sum(value.reshape(size // 8, 8, both), axis=0)

    weight = sweep(0, rows, 32, exp_step, jnp.zeros((8, both), F32))
    weight = jnp.sum(weight, axis=0, keepdims=True)

    own_rows = CORES * sub
    for i in range(RING):
        for s in range(steps):
            part = tiles[s, i, pl.ds(core * CORES, CORES)].reshape(own_rows, tokens)
            hn[i, s * tokens : (s + 1) * tokens, :] = part.T
    for copy in swap_h:
        copy.wait()
    for i in range(RING):
        for s in range(steps):
            part = tiles[steps, i, s * CORES : (s + 1) * CORES].reshape(own_rows, tokens)
            hn[i, both + s * tokens : both + (s + 1) * tokens, :] = part.T

    def widen_in(i):
        part = in_at(i)[...].astype(F32)
        for c in range(lane_parts):
            floats[c, pl.ds(pl.multiple_of(i * slots, 16), slots), :] = part[:, c * 128 : (c + 1) * 128]

    widen_in(tensor)

    def arrived(i, _):
        sent(i).wait()
        widen_in((tensor + PARTS - i) % PARTS)
        return 0

    lax.fori_loop(1, PARTS, arrived, 0)
    pick(lambda j: place_s[0, j], rows)
    if rows > block:
        for c in range(lane_parts):
            picked[c, block:rows, :] = jnp.zeros((rows - block, 128), F32)

    def mass_step(at, size, a):
        return a + jnp.sum(joined(at, size).reshape(size // 8, 8, tokens), axis=0)

    mass_here = sweep(0, rows, 96, mass_step, jnp.zeros((8, tokens), F32))
    mass_here = jnp.sum(mass_here, axis=0, keepdims=True)

    row8 = lax.broadcasted_iota(I32, (8, both), 0)
    mass_wide = jnp.concatenate([mass_here] * steps, axis=1)
    ex2[tensor] = jnp.where(row8 == 0, top, jnp.where(row8 == 1, weight, jnp.where(row8 == 2, mass_wide, 0.0)))
    second = [
        remote(ex2.at[tensor], ex2.at[tensor], ex_send.at[1, i], ex_recv.at[1, i], group_peer(i))
        for i in range(1, PARTS)
    ]
    for copy in second:
        copy.start()

    scales = [LOSS_SCALE * STEP_DECAY**s for s in range(steps)]

    def shift(value, step):
        if step == 0:
            return value
        lane = lax.broadcasted_iota(I32, value.shape, 1)
        return jnp.where(lane < tokens - step, pltpu.roll(value, tokens - step, 1), 0.0)

    def shift_step(at, size, _):
        value = joined(at, size)
        for s in range(1, steps):
            moved[s - 1, pl.ds(at, size), :] = scales[s] * shift(value, s)
        return 0

    sweep(0, rows, 96, shift_step, 0)
    for copy in second:
        copy.wait()
    tops = [ex2[i, 0:1, :] for i in range(PARTS)]
    top_all = functools.reduce(jnp.maximum, tops)
    weight_all = sum(ex2[i, 1:2, :] * jnp.exp(tops[i] - top_all) for i in range(PARTS))
    mass = sum(ex2[i, 2:3, 0:tokens] for i in range(PARTS))

    factor = jnp.exp(top - top_all) / weight_all
    coefs = []
    for s in range(steps):
        mass_of = shift(jnp.broadcast_to(mass, (8, tokens)), s)[0:1, :]
        coefs.append(scales[s] * mass_of * factor[:, s * tokens : (s + 1) * tokens])

    def slope_step(at, size, _):
        for s in range(steps):
            lanes = slice(s * tokens, (s + 1) * tokens)
            prob = moved[s - 1, pl.ds(at, size), :] if s else scales[0] * joined(at, size)
            value = expo[pl.ds(at, size), lanes] * coefs[s] - prob
            sl[pl.ds(at, size), lanes] = value.astype(BF16)
        return 0

    swaps = []
    for n, (at, size) in enumerate(pieces_of(rows)):
        sweep(at, at + size, 96, slope_step, 0)
        swaps.append(
            remote(
                sl.at[pl.ds(at, size), pl.ds(0, both)],
                sl.at[pl.ds(at, size), pl.ds(both, both)],
                pair_send.at[n],
                pair_recv.at[n],
                partner,
            )
        )
        swaps[-1].start()

    def link(n, src, dst, device):
        return remote(src, dst, ring_send.at[n], ring_recv.at[n], device)

    cuts = pieces_of(rows)
    half = rows // 2

    def head_part(by, at, size):
        return jnp.dot(sl[at : at + size, :], hn[(x + by) % RING], preferred_element_type=F32)

    def x_send(slot, by, h, into, to, base, far=None, swapped=()):
        copies = []
        for n in range(2):
            at, size = cuts[2 * h + n]
            for copy in swapped[n : n + 1]:
                copy.wait()
            value = head_part(by, at, size)
            spot = pl.ds(at - h * half, size)
            if far is not None:
                value = value + x_far[far, spot, :].astype(F32)
            x_out[slot, spot, :] = value.astype(BF16)
            copies.append(link(base + n, x_out.at[slot, spot], into.at[spot], x_peer(to)))
            copies[-1].start()
        return copies

    far_r = x_send(0, 2, 0, x_far.at[0], 1, 0, swapped=swaps[:2])
    far_l = x_send(1, 2, 1, x_far.at[1], RING - 1, 2, swapped=swaps[2:])
    free_r = x_send(2, 1, 1, x_in.at[1], 1, 4)
    free_l = x_send(3, RING - 1, 0, x_in.at[2], RING - 1, 6)

    for at in range(0, rows, 128):
        size = min(128, rows - at)
        flat[:, at : at + size] = sl[at : at + size, 0:both].T

    def term_step(i):
        w_again(i).wait()
        value = jnp.dot(flat[:, 0:block], w_buf[i % 2], preferred_element_type=F32)
        first = w_row(i) * chunk
        flipped = value.T
        for lane in range(both // 128):
            spot = pl.ds(pl.multiple_of(lane % lane_parts * PARTS * sub + first, chunk), chunk)
            floats[lane // lane_parts, spot, :] = flipped[:, lane * 128 : (lane + 1) * 128]
        if i + 2 < count:
            w_again(i + 2).start()

    pair_of = RING // 2

    def spot_of(n, c, first, size):
        return pl.ds(pl.multiple_of((c * PARTS + n) * sub + first, 32), size)

    def term(s, n, first=0, size=sub):
        return jnp.concatenate([floats[s, spot_of(n, c, first, size), :] for c in range(lane_parts)], axis=1)

    def term_add(s, n, more):
        for c in range(lane_parts):
            spot = spot_of(n, c, 0, sub)
            floats[s, spot, :] = floats[s, spot, :] + more[:, c * 128 : (c + 1) * 128]

    def p_term(by, n):
        return term(0, ((z + by) % RING) * RING + n)

    def q_term(by, n):
        return term(1, n * RING + (y + by) % RING)

    class Blocks:
        def __init__(self, first, halves):
            self.first, self.halves = first, halves

        def ref(self, slot, n=None):
            if self.halves:
                at = self.first + slot // 2
                return tiles.at[at // PARTS, at // RING % RING, at % RING, pl.ds(slot % 2 * (sub // 2), sub // 2)]
            at = self.first + 2 * slot
            group = tiles.at[at // PARTS, at // RING % RING]
            return group.at[pl.ds(at % RING, 2)] if n is None else group.at[at % RING + n]

        def __getitem__(self, key):
            return self.ref(*key)[...]

    p_out, p_far, p_in = Blocks(0, False), Blocks(12, False), Blocks(16, False)
    q_out, q_far, q_in = Blocks(24, False), Blocks(36, False), Blocks(40, False)
    p2_out, p2_far, p2_in = Blocks(48, True), Blocks(51, True), Blocks(52, True)
    q2_out, q2_far, q2_in = Blocks(54, True), Blocks(57, True), Blocks(58, True)

    def ring_sum(part, out, far, into, peer, base):
        def put(slot, by, h, extra=None):
            for n, value in enumerate(part(by, h)):
                if extra is not None:
                    value = value + far[extra, n].astype(F32)
                out.ref(slot, n)[...] = value.astype(BF16)

        def start(n, slot, dst, by):
            copy = link(base + n, out.ref(slot), dst, peer(by))
            copy.start()
            return copy

        held = {}

        def begin():
            put(0, 2, 0)
            held["a"] = start(0, 0, far.ref(0), 1)
            put(1, 2, 1)
            held["b"] = start(1, 1, far.ref(1), RING - 1)

        def free():
            put(3, 1, 1)
            held["c"] = start(2, 3, into.ref(1), 1)
            put(4, RING - 1, 0)
            held["d"] = start(3, 4, into.ref(2), RING - 1)

        def late():
            held["a"].wait()
            put(2, 1, 0, 0)
            held["e"] = start(4, 2, into.ref(0), 1)
            held["b"].wait()
            put(5, RING - 1, 1, 1)
            held["f"] = start(5, 5, into.ref(3), RING - 1)

        def end():
            for name in "cdef":
                held[name].wait()

        return begin, free, late, end

    def p_part(by, h):
        return [p_term(by, h * pair_of + n) for n in range(pair_of)]

    def q_part(by, h):
        return [q_term(by, h * pair_of + n) for n in range(pair_of)]

    p_begin, p_free, p_late, p_end = ring_sum(p_part, p_out, p_far, p_in, z_peer, 12)
    q_begin, q_free, q_late, q_end = ring_sum(q_part, q_out, q_far, q_in, y_peer, 18)
    for i in range(count):
        term_step(i)
        if i + 1 == per:
            p_begin()
        if i + 1 == 3 * per:
            p_free()
    q_begin()
    q_free()
    p_late()
    q_late()

    for copy in far_r:
        copy.wait()
    dep_r = x_send(0, 1, 0, x_in.at[0], 1, 8, far=0)
    for copy in far_l:
        copy.wait()
    dep_l = x_send(1, RING - 1, 1, x_in.at[3], RING - 1, 10, far=1)

    for at, size in cuts:
        keep = min(size, block - at)
        gw_ref[at : at + keep, :] = head_part(0, at, size)[0:keep]

    p_end()
    for n in range(RING):
        got = p_in[n // pair_of, n % pair_of].astype(F32) + p_in[2 + n // pair_of, n % pair_of].astype(F32)
        term_add(0, z * RING + n, got)
    q_end()
    for n in range(RING):
        got = q_in[n // pair_of, n % pair_of].astype(F32) + q_in[2 + n // pair_of, n % pair_of].astype(F32)
        term_add(1, n * RING + y, got)

    cut = sub // 2

    def p2_part(by, h):
        return [term(0, z * RING + (y + by) % RING, h * cut, cut)]

    def q2_part(by, h):
        return [term(1, ((z + by) % RING) * RING + y, h * cut, cut)]

    p2 = ring_sum(p2_part, p2_out, p2_far, p2_in, y_peer, 24)
    q2 = ring_sum(q2_part, q2_out, q2_far, q2_in, z_peer, 30)
    for stage in range(4):
        p2[stage]()
        q2[stage]()
    for s, into in enumerate((p2_in, q2_in)):
        for h in range(2):
            value = term(s, tensor, h * cut, cut)
            value = value + into[h, 0].astype(F32) + into[2 + h, 0].astype(F32)
            gh_ref[s, h * cut : (h + 1) * cut, :] = value.astype(BF16)

    def add_in(at, size, h):
        to = at + h * half
        got = x_in[h, pl.ds(at, size), :].astype(F32) + x_in[2 + h, pl.ds(at, size), :].astype(F32)
        keep = min(size, block - to)
        gw_ref[to : to + keep, :] = gw_ref[to : to + keep, :] + got[0:keep]

    for h, from_left, from_right in ((0, dep_r, free_l), (1, free_r, dep_l)):
        for n in range(2):
            from_left[n].wait()
            from_right[n].wait()
            at, size = cuts[2 * h + n]
            for i in range(0, size, 16):
                add_in(at - h * half + i, 16, h)


def both_gradients(hid, ids, logits, w, slots):
    steps, sub, tokens = hid.shape
    parts, block = ids.shape
    shard = logits.shape[0]
    both = steps * tokens
    rows = ceil_to(block, 32)
    wide = ceil_to(block, 256)
    width = CORES * sub
    lane_parts = tokens // 128
    half = rows // 2
    depth = max(ceil_to(max(shard, parts * slots), 32), lane_parts * parts * sub)
    vmem = pl.BlockSpec(memory_space=pltpu.VMEM)
    hbm = pl.BlockSpec(memory_space=pl.ANY)
    dma = pltpu.SemaphoreType.DMA
    return pl.pallas_call(
        functools.partial(kernel, (steps, tokens, block, rows, slots)),
        out_shape=(
            jax.ShapeDtypeStruct((steps, sub, tokens), BF16),
            jax.ShapeDtypeStruct((block, width), F32),
        ),
        in_specs=[vmem, vmem, hbm, hbm],
        out_specs=(vmem, vmem),
        scratch_shapes=[
            pltpu.VMEM((2 + steps, RING, RING, sub, tokens), BF16),
            pltpu.VMEM((shard, tokens), BF16),
            pltpu.VMEM((lane_parts, depth, 128), F32),
            pltpu.VMEM((RING, CORES * both, width), BF16),
            pltpu.VMEM((rows, CORES * both), BF16),
            pltpu.VMEM((2, block, 2 * sub), BF16),
            pltpu.VMEM((lane_parts, rows, 128), F32),
            pltpu.VMEM((rows, both), F32),
            pltpu.VMEM((steps - 1, rows, tokens), F32),
            pltpu.VMEM((both, ceil_to(rows, 128)), BF16),
            pltpu.VMEM((3, parts, wide), F32),
            pltpu.VMEM((parts, ceil_to(slots, 128)), I32),
            pltpu.VMEM((8, wide), I32),
            pltpu.VMEM((parts, 8, tokens), F32),
            pltpu.VMEM((parts, 8, both), F32),
            pltpu.VMEM((4, half, width), BF16),
            pltpu.VMEM((2, half, width), BF16),
            pltpu.VMEM((4, half, width), BF16),
            pltpu.SMEM((parts, ceil_to(slots, 128)), I32),
            pltpu.SMEM((8, wide), I32),
            dma((24,)),
            dma((24,)),
            dma((parts,)),
            dma((parts,)),
            dma((2, parts)),
            dma((2, parts)),
            dma((6,)),
            dma((6,)),
            dma((2,)),
            dma((3,)),
            dma((36,)),
            dma((36,)),
        ],
        compiler_params=pltpu.CompilerParams(
            collective_id=2, has_side_effects=True, vmem_limit_bytes=63 * 2**20
        ),
        name="both_gradients",
    )(hid, ids, logits, w)


def hand_on_kernel(gh_in, gw_in, gh_out, gw_out):
    gh_out[...] = gh_in[...]
    gw_out[...] = gw_in[...]


def hand_on(gh, gw):
    steps, sub, tokens = gh.shape
    block, width = gw.shape
    blocks = 4
    size = ceil_to(-(-block // blocks), 8)
    gh_spec = pl.BlockSpec((steps, sub // blocks, tokens), lambda i: (0, i, 0))
    gw_spec = pl.BlockSpec((size, width), lambda i: (i, 0))
    return pl.pallas_call(
        hand_on_kernel,
        grid=(blocks,),
        out_shape=(jax.ShapeDtypeStruct(gh.shape, gh.dtype), jax.ShapeDtypeStruct(gw.shape, gw.dtype)),
        in_specs=[gh_spec, gw_spec],
        out_specs=(gh_spec, gw_spec),
        name="hand_on",
    )(gh, gw)


def per_device(hidden, draft_head, target_logits, draft_to_target):
    steps, tokens, _ = hidden.shape
    block = draft_to_target.shape[0] // PARTS
    heavy = block // 8
    bound = heavy + (block - heavy + PARTS - 1) // PARTS
    slots = ceil_to(bound, 16)
    w = draft_head.T
    ids = draft_to_target.reshape(PARTS, block)
    gh, gw = hand_on(*both_gradients(hidden.transpose(0, 2, 1), ids, target_logits.T, w, slots))
    return gh.transpose(0, 2, 1), gw.T


def solution(mesh):
    in_specs = (P(None, "dp", "tensor"), P(None, "tensor"), P("dp", "tensor"), P())
    out_specs = (P(None, "dp", "tensor"), P("dp", "tensor"))
    return jax.shard_map(
        per_device, mesh=mesh, in_specs=in_specs, out_specs=out_specs, check_vma=False
    )
```

```python
import functools

import jax
import jax.numpy as jnp
from jax import lax
from jax.experimental import pallas as pl
from jax.experimental.pallas import tpu as pltpu
from jax.sharding import PartitionSpec as P

LOSS_SCALE = 256.0
STEP_DECAY = 0.8
MESH = pl.DeviceIdType.MESH
F32 = jnp.float32
BF16 = jnp.bfloat16
I32 = jnp.int32
RING = 4
CORES = 2
PARTS = RING * RING
LOW = -3.0e38
HELD = 4
NT = (((1,), (1,)), ((), ()))


def ceil_to(value, unit):
    return (value + unit - 1) // unit * unit


def places():
    dp = lax.axis_index("dp")
    tensor = lax.axis_index("tensor")
    x, core = dp // CORES, dp % CORES
    z, y = tensor // RING, tensor % RING
    return dp, tensor, x, core, z, y


def sweep(first, last, size, step, carry):
    full = (last - first) // size

    def go(i, value):
        return step(pl.multiple_of(first + i * size, 16), size, value)

    carry = lax.fori_loop(0, full, go, carry)
    if first + full * size < last:
        carry = step(first + full * size, last - first - full * size, carry)
    return carry


def remote(src, dst, send, recv, device):
    return pltpu.make_async_remote_copy(
        src_ref=src, dst_ref=dst, send_sem=send, recv_sem=recv, device_id=device, device_id_type=MESH
    )


def pieces_of(rows):
    half = rows // 2
    first = ceil_to(half // 2, 16)
    return [(0, first), (first, half - first), (half, first), (half + first, half - first)]


def kernel(
    sizes,
    hid_ref,
    ids_ref,
    logits_hbm,
    w_ref,
    gh_ref,
    gw_ref,
    tiles,
    arena,
    floats,
    hn,
    sl,
    w_buf,
    picked,
    expo,
    flat,
    rank_v,
    count_v,
    tab_v,
    place_v,
    ex1,
    ex2,
    x_out,
    x_far,
    x_in,
    tab_s,
    place_s,
    ag_send,
    ag_recv,
    a2a_send,
    a2a_recv,
    ex_send,
    ex_recv,
    pair_send,
    pair_recv,
    w_sem,
    s_sem,
    ring_send,
    ring_recv,
):
    logits_in = pltpu.make_async_copy(logits_hbm, arena, s_sem.at[2])
    logits_in.start()
    steps, tokens, block, rows, slots = sizes
    shard = arena.shape[0]
    sub = hid_ref.shape[1]
    both = steps * tokens
    wide = ceil_to(block, 256)
    lane_parts = tokens // 128
    dp, tensor, x, core, z, y = places()
    partner = (x * CORES + 1 - core, tensor)

    def x_peer(by):
        return (((x + by) % RING) * CORES + core, tensor)

    def z_peer(by):
        return (dp, ((z + by) % RING) * RING + y)

    def y_peer(by):
        return (dp, z * RING + (y + by) % RING)

    def group_peer(i):
        return (dp, (tensor + i) % PARTS)

    chunk = w_buf.shape[2]

    def w_copy(i):
        return pltpu.make_async_copy(w_ref.at[:, pl.ds(i * chunk, chunk)], w_buf.at[i % 2], w_sem.at[i % 2])

    w_copy(0).start()
    w_copy(1).start()
    for s in range(steps):
        tiles[s, z, y] = hid_ref[s]

    barrier = pltpu.get_barrier_semaphore()
    for i in range(1, PARTS):
        pl.semaphore_signal(barrier, inc=1, device_id=group_peer(i), device_id_type=MESH)
    pl.semaphore_signal(barrier, inc=1, device_id=partner, device_id_type=MESH)
    for by in (1, RING - 1):
        pl.semaphore_signal(barrier, inc=1, device_id=x_peer(by), device_id_type=MESH)
    pl.semaphore_wait(barrier, PARTS + 2)

    def gather_ring(half, at, peer, base):
        right, left = (at + 1) % RING, (at + RING - 1) % RING

        def copy(n, r, h, by):
            ref = half(r, h)
            return remote(ref, ref, ag_send.at[base + n], ag_recv.at[base + n], peer(by))

        r1 = copy(0, at, 0, 1)
        l1 = copy(1, at, 1, RING - 1)
        r2 = copy(2, at, 1, 1)
        l2 = copy(3, at, 0, RING - 1)
        for c in (r1, l1, r2, l2):
            c.start()

        def pass_on():
            r1.wait()
            r3 = copy(4, left, 0, 1)
            r3.start()
            l1.wait()
            l3 = copy(5, right, 1, RING - 1)
            l3.start()

            def finish():
                for c in (r2, l2, r3, l3):
                    c.wait()

            return finish

        return pass_on

    def half_rows(s, at_z, at_y, h):
        return tiles.at[s, at_z, at_y, pl.ds(h * (sub // 2), sub // 2)]

    two = RING // 2
    p1 = gather_ring(lambda r, h: half_rows(0, z, r, h), y, y_peer, 0)
    q1 = gather_ring(lambda r, h: half_rows(1, r, y, h), z, z_peer, 6)

    def top_rows(at, size, best):
        part = arena[pl.ds(at, size), :].astype(F32)
        return jnp.maximum(best, jnp.max(part.reshape(size // 8, 8, tokens), axis=0))

    logits_in.wait()
    best = sweep(0, shard, 64, top_rows, jnp.full((8, tokens), LOW, F32))
    peak_here = jnp.max(best, axis=0, keepdims=True)

    def exp_rows(at, size, acc):
        part = jnp.exp(arena[pl.ds(at, size), :].astype(F32) - peak_here)
        for c in range(lane_parts):
            floats[c, pl.ds(at, size), :] = part[:, c * 128 : (c + 1) * 128]
        return acc + jnp.sum(part.reshape(size // 8, 8, tokens), axis=0)

    acc = sweep(0, shard, 64, exp_rows, jnp.zeros((8, tokens), F32))
    total_here = jnp.sum(acc, axis=0, keepdims=True)
    row8 = lax.broadcasted_iota(I32, (8, tokens), 0)
    ex1[tensor] = jnp.where(row8 == 0, peak_here, jnp.where(row8 == 1, total_here, 0.0))
    first = [
        remote(ex1.at[tensor], ex1.at[tensor], ex_send.at[0, i], ex_recv.at[0, i], group_peer(i))
        for i in range(1, PARTS)
    ]
    for copy in first:
        copy.start()

    ids = jnp.concatenate([ids_ref[...], jnp.full((PARTS, wide - block), -1, I32)], axis=1)
    local = ids - tensor * shard
    mine = (local >= 0) & (local < shard)
    own = jnp.sum(jnp.where(lax.broadcasted_iota(I32, (PARTS, wide), 0) == tensor, ids, 0), axis=0, keepdims=True)
    start = lax.broadcasted_iota(I32, (PARTS, wide), 0) * shard
    from_owner = (own >= start) & (own < start + shard)
    hits = jnp.concatenate([jnp.where(mine, 1.0, 0.0), jnp.where(from_owner, 1.0, 0.0)], axis=0)
    before = lax.broadcasted_iota(I32, (256, 256), 0)
    after = lax.broadcasted_iota(I32, (256, 256), 1)
    upper = jnp.where(before <= after, 1.0, 0.0).astype(BF16)
    seen = jnp.full((2 * PARTS, 1), -1.0, F32)
    rank_list = []
    for n in range(wide // 256):
        part = hits[:, n * 256 : (n + 1) * 256]
        rank_list.append(jnp.dot(part.astype(BF16), upper, preferred_element_type=F32) + seen)
        seen = seen + jnp.sum(part, axis=1, keepdims=True)
    ranks = jnp.concatenate(rank_list, axis=1)
    count_v[...] = jnp.broadcast_to(seen[:PARTS] + 1.0, count_v.shape)
    owner = lax.broadcasted_iota(I32, (PARTS, wide), 0).astype(F32) * float(slots)
    place = jnp.sum(jnp.where(from_owner, owner + ranks[PARTS:], 0.0), axis=0, keepdims=True)
    place_v[...] = jnp.clip(jnp.broadcast_to(place, (8, wide)).astype(I32), 0, PARTS * slots - 1)
    rank_v[0] = jnp.where(mine, ranks[:PARTS], -1.0)
    rank_v[1] = jnp.where(mine, local - (local & 255), 0).astype(F32)
    rank_v[2] = jnp.where(mine, local & 255, 0).astype(F32)
    to_place = pltpu.make_async_copy(place_v, place_s, s_sem.at[0])
    to_place.start()

    p1_end = p1()
    q1_end = q1()

    slot = (lax.broadcasted_iota(I32, (slots // 16, 16, wide), 0) * 16).astype(F32)
    slot = slot + lax.broadcasted_iota(I32, (slots // 16, 16, wide), 1).astype(F32)
    slot = (slot - 128.0).astype(BF16)
    kind = lax.broadcasted_iota(I32, (8, wide), 0)

    tab_v[...] = jnp.zeros_like(tab_v)

    def table_step(b, _):
        rank = jnp.minimum(rank_v[0, pl.ds(b, 1), :], float(slots)) - 128.0
        rank = jnp.broadcast_to(rank, (16, wide)).astype(BF16)
        info = jnp.where(kind == 0, rank_v[1, pl.ds(b, 1), :], jnp.where(kind == 1, rank_v[2, pl.ds(b, 1), :], 0.0))
        hot = jnp.where(slot == rank[None], jnp.ones((), BF16), jnp.zeros((), BF16)).reshape(slots, wide)
        got = lax.dot_general(info.astype(BF16), hot, NT, preferred_element_type=F32)
        found = (got[0:1, :] + got[1:2, :]).astype(I32)
        tab_v[pl.ds(b, 1), 0:slots] = jnp.clip(found, 0, shard - 1)
        return 0

    lax.fori_loop(0, two, table_step, 0)
    p1_end()
    q1_end()
    p2 = gather_ring(lambda r, h: tiles.at[0, r, pl.ds(h * two, two)], z, z_peer, 12)
    q2 = gather_ring(lambda r, h: tiles.at[1, pl.ds(h * two, two), r], y, y_peer, 18)
    lax.fori_loop(two, PARTS, table_step, 0)
    to_tab = pltpu.make_async_copy(tab_v, tab_s, s_sem.at[1])
    to_tab.start()

    for copy in first:
        copy.wait()
    peaks = [ex1[i, 0:1, :] for i in range(PARTS)]
    peak = functools.reduce(jnp.maximum, peaks)
    total = sum(ex1[i, 1:2, :] * jnp.exp(peaks[i] - peak) for i in range(PARTS))
    share = jnp.exp(peak_here - peak) / total
    to_tab.wait()
    to_place.wait()

    def pick(index_of, first, last):
        def go(i, _):
            got = []
            for r in range(16):
                at = index_of(i * 16 + r)
                got.append([floats[c, pl.ds(at, 1), :] for c in range(lane_parts)])
            for r in range(16):
                for c in range(lane_parts):
                    picked[c, pl.ds(i * 16 + r, 1), :] = got[r][c]
            return 0

        lax.fori_loop(first // 16, last // 16, go, 0)

    def joined(at, size):
        return jnp.concatenate([picked[c, pl.ds(at, size), :] for c in range(lane_parts)], axis=1)

    def out_at(i):
        return arena.at[pl.ds(pl.multiple_of(i * slots, 16), slots)]

    def in_at(i):
        return arena.at[pl.ds(pl.multiple_of((PARTS + i) * slots, 16), slots)]

    def sent(i):
        to = (tensor + i) % PARTS
        return remote(out_at(to), in_at(tensor), a2a_send.at[i], a2a_recv.at[i], (dp, to))

    row_of = lax.broadcasted_iota(I32, (slots, tokens), 0).astype(F32)

    def pick_into(to, ref, mass):
        pick(lambda j: tab_s[to, j], 0, slots)
        value = (joined(0, slots) * share).astype(BF16)
        ref[...] = value
        used = row_of < jnp.concatenate([count_v[pl.ds(to, 1), :]] * lane_parts, axis=1)
        value = jnp.where(used, value.astype(F32), 0.0)
        return mass + jnp.sum(value.reshape(slots // 8, 8, tokens), axis=0)

    def pick_step(i, mass):
        to = (tensor + i) % PARTS
        return pick_into(to, out_at(to), mass)

    def send_step(i, _):
        sent(i).start()
        return 0

    mass_here = lax.fori_loop(1, HELD, pick_step, jnp.zeros((8, tokens), F32))
    p2_end = p2()
    q2_end = q2()
    mass_here = lax.fori_loop(HELD, PARTS, pick_step, mass_here)
    mass_here = jnp.sum(pick_into(tensor, in_at(tensor), mass_here), axis=0, keepdims=True)

    p2_end()
    q2_end()
    lax.fori_loop(1, PARTS, send_step, 0)
    swap_h = [
        remote(
            tiles.at[s, :, pl.ds((1 - core) * CORES, CORES)],
            tiles.at[steps, :, pl.ds(s * CORES, CORES)],
            pair_send.at[4 + s],
            pair_recv.at[4 + s],
            partner,
        )
        for s in range(steps)
    ]
    for copy in swap_h:
        copy.start()

    pieces = PARTS * sub // chunk
    each = chunk // sub
    expo[...] = jnp.zeros((rows, both), F32)

    def score_step(i, _):
        w_copy(i).wait()
        for s in range(steps):
            at = i * each
            h = tiles[s, at // RING, pl.ds(at % RING, each)].reshape(chunk, tokens)
            lanes = slice(s * tokens, (s + 1) * tokens)
            expo[0:block, lanes] += jnp.dot(w_buf[i % 2], h, preferred_element_type=F32)

        @pl.when(i + 2 < pieces)
        def _():
            w_copy(i + 2).start()

        return 0

    lax.fori_loop(0, pieces, score_step, 0)

    per = RING * sub // chunk
    count = RING * per

    def w_row(i):
        order = (2, 1, RING - 1, 0)[i // per]
        return ((z + order) % RING) * per + i % per

    def w_again(i):
        at = pl.multiple_of(w_row(i) * chunk, chunk)
        return pltpu.make_async_copy(w_ref.at[:, pl.ds(at, chunk)], w_buf.at[i % 2], w_sem.at[i % 2])

    w_again(0).start()
    w_again(1).start()
    if rows > block:
        expo[block:rows, :] = jnp.full((rows - block, both), LOW, F32)

    def top_step(at, size, m):
        return jnp.maximum(m, jnp.max(expo[pl.ds(at, size), :].reshape(size // 8, 8, both), axis=0))

    top = sweep(0, rows, 32, top_step, jnp.full((8, both), LOW, F32))
    top = jnp.max(top, axis=0, keepdims=True)

    def exp_step(at, size, a):
        value = jnp.exp(expo[pl.ds(at, size), :] - top)
        expo[pl.ds(at, size), :] = value
        return a + jnp.sum(value.reshape(size // 8, 8, both), axis=0)

    weight = sweep(0, rows, 32, exp_step, jnp.zeros((8, both), F32))
    weight = jnp.sum(weight, axis=0, keepdims=True)

    own_rows = CORES * sub
    for i in range(RING):
        for s in range(steps):
            part = tiles[s, i, pl.ds(core * CORES, CORES)].reshape(own_rows, tokens)
            hn[i, s * tokens : (s + 1) * tokens, :] = part.T
    for copy in swap_h:
        copy.wait()
    for i in range(RING):
        for s in range(steps):
            part = tiles[steps, i, s * CORES : (s + 1) * CORES].reshape(own_rows, tokens)
            hn[i, both + s * tokens : both + (s + 1) * tokens, :] = part.T

    row8 = lax.broadcasted_iota(I32, (8, both), 0)
    mass_wide = jnp.concatenate([mass_here] * steps, axis=1)
    ex2[tensor] = jnp.where(row8 == 0, top, jnp.where(row8 == 1, weight, jnp.where(row8 == 2, mass_wide, 0.0)))
    second = [
        remote(ex2.at[tensor], ex2.at[tensor], ex_send.at[1, i], ex_recv.at[1, i], group_peer(i))
        for i in range(1, PARTS)
    ]
    for copy in second:
        copy.start()

    def widen_in(i):
        part = in_at(i)[...].astype(F32)
        for c in range(lane_parts):
            floats[c, pl.ds(pl.multiple_of(i * slots, 16), slots), :] = part[:, c * 128 : (c + 1) * 128]

    widen_in(tensor)

    def arrived(i, _):
        sent(i).wait()
        widen_in((tensor + PARTS - i) % PARTS)
        return 0

    lax.fori_loop(1, PARTS, arrived, 0)
    for copy in second:
        copy.wait()
    tops = [ex2[i, 0:1, :] for i in range(PARTS)]
    top_all = functools.reduce(jnp.maximum, tops)
    weight_all = sum(ex2[i, 1:2, :] * jnp.exp(tops[i] - top_all) for i in range(PARTS))
    mass = sum(ex2[i, 2:3, 0:tokens] for i in range(PARTS))

    scales = [LOSS_SCALE * STEP_DECAY**s for s in range(steps)]

    def shift(value, step):
        if step == 0:
            return value
        lane = lax.broadcasted_iota(I32, value.shape, 1)
        return jnp.where(lane < tokens - step, pltpu.roll(value, tokens - step, 1), 0.0)

    factor = jnp.exp(top - top_all) / weight_all
    coefs = []
    for s in range(steps):
        mass_of = shift(jnp.broadcast_to(mass, (8, tokens)), s)[0:1, :]
        coefs.append(scales[s] * mass_of * factor[:, s * tokens : (s + 1) * tokens])

    def slope_step(at, size, _):
        prob = joined(at, size)
        for s in range(steps):
            lanes = slice(s * tokens, (s + 1) * tokens)
            value = expo[pl.ds(at, size), lanes] * coefs[s] - scales[s] * shift(prob, s)
            sl[pl.ds(at, size), lanes] = value.astype(BF16)
        return 0

    def link(n, src, dst, device):
        return remote(src, dst, ring_send.at[n], ring_recv.at[n], device)

    cuts = pieces_of(rows)
    half = rows // 2

    def head_part(by, at, size):
        return jnp.dot(sl[at : at + size, :], hn[(x + by) % RING], preferred_element_type=F32)

    def x_piece(slot, by, cut, into, to, n, far=None):
        at, size = cuts[cut]
        value = head_part(by, at, size)
        spot = pl.ds(at - cut // 2 * half, size)
        if far is not None:
            value = value + x_far[far, spot, :].astype(F32)
        x_out[slot, spot, :] = value.astype(BF16)
        copy = link(n, x_out.at[slot, spot], into.at[spot], x_peer(to))
        copy.start()
        return copy

    def x_send(slot, by, h, into, to, base, far=None):
        return [x_piece(slot, by, 2 * h + n, into, to, base + n, far) for n in range(2)]

    far_of = [None] * 4
    waiting = []

    def send_far():
        cut, copy = waiting.pop()
        copy.wait()
        h = cut // 2
        far_of[cut] = x_piece(h, 2, cut, x_far.at[h], (1, RING - 1)[h], cut)

    for cut in (0, 2, 1, 3):
        at, size = cuts[cut]
        pick(lambda j: place_s[0, j], at, at + size)
        if at + size > block:
            for c in range(lane_parts):
                picked[c, block : at + size, :] = jnp.zeros((at + size - block, 128), F32)
        sweep(at, at + size, 96, slope_step, 0)
        swap = remote(
            sl.at[pl.ds(at, size), pl.ds(0, both)],
            sl.at[pl.ds(at, size), pl.ds(both, both)],
            pair_send.at[cut],
            pair_recv.at[cut],
            partner,
        )
        swap.start()
        if waiting:
            send_far()
        waiting.append((cut, swap))
    send_far()
    far_r, far_l = far_of[:2], far_of[2:]
    free_r = x_send(2, 1, 1, x_in.at[1], 1, 4)
    free_l = x_send(3, RING - 1, 0, x_in.at[2], RING - 1, 6)

    for at in range(0, rows, 128):
        size = min(128, rows - at)
        flat[:, at : at + size] = sl[at : at + size, 0:both].T

    def term_step(i):
        w_again(i).wait()
        value = jnp.dot(flat[:, 0:block], w_buf[i % 2], preferred_element_type=F32)
        first = w_row(i) * chunk
        flipped = value.T
        for lane in range(both // 128):
            spot = pl.ds(pl.multiple_of(lane % lane_parts * PARTS * sub + first, chunk), chunk)
            floats[lane // lane_parts, spot, :] = flipped[:, lane * 128 : (lane + 1) * 128]
        if i + 2 < count:
            w_again(i + 2).start()

    pair_of = RING // 2

    def spot_of(n, c, first, size):
        return pl.ds(pl.multiple_of((c * PARTS + n) * sub + first, 32), size)

    def term(s, n, first=0, size=sub):
        return jnp.concatenate([floats[s, spot_of(n, c, first, size), :] for c in range(lane_parts)], axis=1)

    def term_add(s, n, more):
        for c in range(lane_parts):
            spot = spot_of(n, c, 0, sub)
            floats[s, spot, :] = floats[s, spot, :] + more[:, c * 128 : (c + 1) * 128]

    def p_term(by, n):
        return term(0, ((z + by) % RING) * RING + n)

    def q_term(by, n):
        return term(1, n * RING + (y + by) % RING)

    class Blocks:
        def __init__(self, first, halves):
            self.first, self.halves = first, halves

        def ref(self, slot, n=None):
            if self.halves:
                at = self.first + slot // 2
                return tiles.at[at // PARTS, at // RING % RING, at % RING, pl.ds(slot % 2 * (sub // 2), sub // 2)]
            at = self.first + 2 * slot
            group = tiles.at[at // PARTS, at // RING % RING]
            return group.at[pl.ds(at % RING, 2)] if n is None else group.at[at % RING + n]

        def __getitem__(self, key):
            return self.ref(*key)[...]

    p_out, p_far, p_in = Blocks(0, False), Blocks(12, False), Blocks(16, False)
    q_out, q_far, q_in = Blocks(24, False), Blocks(36, False), Blocks(40, False)
    p2_out, p2_far, p2_in = Blocks(48, True), Blocks(51, True), Blocks(52, True)
    q2_out, q2_far, q2_in = Blocks(54, True), Blocks(57, True), Blocks(58, True)

    def ring_sum(part, out, far, into, peer, base):
        def put(slot, by, h, extra=None):
            for n, value in enumerate(part(by, h)):
                if extra is not None:
                    value = value + far[extra, n].astype(F32)
                out.ref(slot, n)[...] = value.astype(BF16)

        def start(n, slot, dst, by):
            copy = link(base + n, out.ref(slot), dst, peer(by))
            copy.start()
            return copy

        held = {}

        def begin():
            put(0, 2, 0)
            held["a"] = start(0, 0, far.ref(0), 1)
            put(1, 2, 1)
            held["b"] = start(1, 1, far.ref(1), RING - 1)

        def free():
            put(3, 1, 1)
            held["c"] = start(2, 3, into.ref(1), 1)
            put(4, RING - 1, 0)
            held["d"] = start(3, 4, into.ref(2), RING - 1)

        def late():
            held["a"].wait()
            put(2, 1, 0, 0)
            held["e"] = start(4, 2, into.ref(0), 1)
            held["b"].wait()
            put(5, RING - 1, 1, 1)
            held["f"] = start(5, 5, into.ref(3), RING - 1)

        def end():
            for name in "cdef":
                held[name].wait()

        return begin, free, late, end

    def p_part(by, h):
        return [p_term(by, h * pair_of + n) for n in range(pair_of)]

    def q_part(by, h):
        return [q_term(by, h * pair_of + n) for n in range(pair_of)]

    p_begin, p_free, p_late, p_end = ring_sum(p_part, p_out, p_far, p_in, z_peer, 12)
    q_begin, q_free, q_late, q_end = ring_sum(q_part, q_out, q_far, q_in, y_peer, 18)
    for i in range(count):
        term_step(i)
        if i + 1 == per:
            p_begin()
        if i + 1 == 3 * per:
            p_free()
    q_begin()
    q_free()
    p_late()
    q_late()

    for copy in far_r:
        copy.wait()
    dep_r = x_send(0, 1, 0, x_in.at[0], 1, 8, far=0)
    for copy in far_l:
        copy.wait()
    dep_l = x_send(1, RING - 1, 1, x_in.at[3], RING - 1, 10, far=1)

    for at, size in cuts:
        keep = min(size, block - at)
        gw_ref[at : at + keep, :] = head_part(0, at, size)[0:keep]

    p_end()
    for n in range(RING):
        got = p_in[n // pair_of, n % pair_of].astype(F32) + p_in[2 + n // pair_of, n % pair_of].astype(F32)
        term_add(0, z * RING + n, got)
    q_end()
    for n in range(RING):
        got = q_in[n // pair_of, n % pair_of].astype(F32) + q_in[2 + n // pair_of, n % pair_of].astype(F32)
        term_add(1, n * RING + y, got)

    cut = sub // 2

    def p2_part(by, h):
        return [term(0, z * RING + (y + by) % RING, h * cut, cut)]

    def q2_part(by, h):
        return [term(1, ((z + by) % RING) * RING + y, h * cut, cut)]

    p2 = ring_sum(p2_part, p2_out, p2_far, p2_in, y_peer, 24)
    q2 = ring_sum(q2_part, q2_out, q2_far, q2_in, z_peer, 30)
    for stage in range(4):
        p2[stage]()
        q2[stage]()
    for s, into in enumerate((p2_in, q2_in)):
        for h in range(2):
            value = term(s, tensor, h * cut, cut)
            value = value + into[h, 0].astype(F32) + into[2 + h, 0].astype(F32)
            gh_ref[s, h * cut : (h + 1) * cut, :] = value.astype(BF16)

    def add_in(at, size, h):
        to = at + h * half
        got = x_in[h, pl.ds(at, size), :].astype(F32) + x_in[2 + h, pl.ds(at, size), :].astype(F32)
        keep = min(size, block - to)
        gw_ref[to : to + keep, :] = gw_ref[to : to + keep, :] + got[0:keep]

    for h, from_left, from_right in ((0, dep_r, free_l), (1, free_r, dep_l)):
        for n in range(2):
            from_left[n].wait()
            from_right[n].wait()
            at, size = cuts[2 * h + n]
            for i in range(0, size, 16):
                add_in(at - h * half + i, 16, h)


def both_gradients(hid, ids, logits, w, slots):
    steps, sub, tokens = hid.shape
    parts, block = ids.shape
    shard = logits.shape[0]
    both = steps * tokens
    rows = ceil_to(block, 32)
    wide = ceil_to(block, 256)
    width = CORES * sub
    lane_parts = tokens // 128
    half = rows // 2
    depth = max(ceil_to(max(shard, parts * slots), 32), lane_parts * parts * sub)
    vmem = pl.BlockSpec(memory_space=pltpu.VMEM)
    hbm = pl.BlockSpec(memory_space=pl.ANY)
    dma = pltpu.SemaphoreType.DMA
    return pl.pallas_call(
        functools.partial(kernel, (steps, tokens, block, rows, slots)),
        out_shape=(
            jax.ShapeDtypeStruct((steps, sub, tokens), BF16),
            jax.ShapeDtypeStruct((block, width), F32),
        ),
        in_specs=[vmem, vmem, hbm, hbm],
        out_specs=(vmem, vmem),
        scratch_shapes=[
            pltpu.VMEM((2 + steps, RING, RING, sub, tokens), BF16),
            pltpu.VMEM((shard, tokens), BF16),
            pltpu.VMEM((lane_parts, depth, 128), F32),
            pltpu.VMEM((RING, CORES * both, width), BF16),
            pltpu.VMEM((rows, CORES * both), BF16),
            pltpu.VMEM((2, block, 2 * sub), BF16),
            pltpu.VMEM((lane_parts, rows, 128), F32),
            pltpu.VMEM((rows, both), F32),
            pltpu.VMEM((both, ceil_to(rows, 128)), BF16),
            pltpu.VMEM((3, parts, wide), F32),
            pltpu.VMEM((parts, 128), F32),
            pltpu.VMEM((parts, ceil_to(slots, 128)), I32),
            pltpu.VMEM((8, wide), I32),
            pltpu.VMEM((parts, 8, tokens), F32),
            pltpu.VMEM((parts, 8, both), F32),
            pltpu.VMEM((4, half, width), BF16),
            pltpu.VMEM((2, half, width), BF16),
            pltpu.VMEM((4, half, width), BF16),
            pltpu.SMEM((parts, ceil_to(slots, 128)), I32),
            pltpu.SMEM((8, wide), I32),
            dma((24,)),
            dma((24,)),
            dma((parts,)),
            dma((parts,)),
            dma((2, parts)),
            dma((2, parts)),
            dma((6,)),
            dma((6,)),
            dma((2,)),
            dma((3,)),
            dma((36,)),
            dma((36,)),
        ],
        compiler_params=pltpu.CompilerParams(
            collective_id=2, has_side_effects=True, vmem_limit_bytes=63 * 2**20
        ),
        name="both_gradients",
    )(hid, ids, logits, w)


def hand_on_kernel(gh_in, gw_in, gh_out, gw_out, sem):
    block = gw_in.shape[0]
    size = ceil_to(-(-block // 4), 8)
    copies = [pltpu.make_async_copy(gh_in, gh_out, sem.at[0])]
    for n in range(4):
        rows = pl.ds(n * size, min(size, block - n * size))
        copies.append(pltpu.make_async_copy(gw_in.at[rows], gw_out.at[rows], sem.at[1 + n]))
    for copy in copies:
        copy.start()
    for copy in copies:
        copy.wait()


def hand_on(gh, gw):
    hbm = pl.BlockSpec(memory_space=pl.ANY)
    return pl.pallas_call(
        hand_on_kernel,
        out_shape=(jax.ShapeDtypeStruct(gh.shape, gh.dtype), jax.ShapeDtypeStruct(gw.shape, gw.dtype)),
        in_specs=[hbm, hbm],
        out_specs=(hbm, hbm),
        scratch_shapes=[pltpu.SemaphoreType.DMA((5,))],
        name="hand_on",
    )(gh, gw)


def per_device(hidden, draft_head, target_logits, draft_to_target):
    steps, tokens, _ = hidden.shape
    block = draft_to_target.shape[0] // PARTS
    heavy = block // 8
    bound = heavy + (block - heavy + PARTS - 1) // PARTS
    slots = ceil_to(bound, 16)
    w = draft_head.T
    ids = draft_to_target.reshape(PARTS, block)
    gh, gw = hand_on(*both_gradients(hidden.transpose(0, 2, 1), ids, target_logits.T, w, slots))
    return gh.transpose(0, 2, 1), gw.T


def solution(mesh):
    in_specs = (P(None, "dp", "tensor"), P(None, "tensor"), P("dp", "tensor"), P())
    out_specs = (P(None, "dp", "tensor"), P("dp", "tensor"))
    return jax.shard_map(
        per_device, mesh=mesh, in_specs=in_specs, out_specs=out_specs, check_vma=False
    )
```

```python
import functools

import jax
import jax.numpy as jnp
from jax import lax
from jax.experimental import pallas as pl
from jax.experimental.pallas import tpu as pltpu
from jax.sharding import PartitionSpec as P

LOSS_SCALE = 256.0
STEP_DECAY = 0.8
MESH = pl.DeviceIdType.MESH
F32 = jnp.float32
BF16 = jnp.bfloat16
I32 = jnp.int32
RING = 4
CORES = 2
PARTS = RING * RING
LOW = -3.0e38
HELD = 4
NT = (((1,), (1,)), ((), ()))


def ceil_to(value, unit):
    return (value + unit - 1) // unit * unit


def places():
    dp = lax.axis_index("dp")
    tensor = lax.axis_index("tensor")
    x, core = dp // CORES, dp % CORES
    z, y = tensor // RING, tensor % RING
    return dp, tensor, x, core, z, y


def sweep(first, last, size, step, carry):
    full = (last - first) // size

    def go(i, value):
        return step(pl.multiple_of(first + i * size, 16), size, value)

    carry = lax.fori_loop(0, full, go, carry)
    if first + full * size < last:
        carry = step(first + full * size, last - first - full * size, carry)
    return carry


def remote(src, dst, send, recv, device):
    return pltpu.make_async_remote_copy(
        src_ref=src, dst_ref=dst, send_sem=send, recv_sem=recv, device_id=device, device_id_type=MESH
    )


def pieces_of(rows):
    half = rows // 2
    first = ceil_to(half // 2, 16)
    return [(0, first), (first, half - first), (half, first), (half + first, half - first)]


def kernel(
    sizes,
    hid_ref,
    ids_ref,
    logits_hbm,
    w_ref,
    gh_ref,
    gw_ref,
    tiles,
    arena,
    floats,
    hn,
    sl,
    w_buf,
    picked,
    expo,
    flat,
    rank_v,
    count_v,
    tab_v,
    place_v,
    ex1,
    ex2,
    x_out,
    x_far,
    x_in,
    tab_s,
    place_s,
    ag_send,
    ag_recv,
    a2a_send,
    a2a_recv,
    ex_send,
    ex_recv,
    pair_send,
    pair_recv,
    w_sem,
    s_sem,
    ring_send,
    ring_recv,
):
    logits_in = pltpu.make_async_copy(logits_hbm, arena, s_sem.at[2])
    logits_in.start()
    steps, tokens, block, rows, slots = sizes
    shard = arena.shape[0]
    sub = hid_ref.shape[1]
    both = steps * tokens
    wide = ceil_to(block, 256)
    lane_parts = tokens // 128
    dp, tensor, x, core, z, y = places()
    partner = (x * CORES + 1 - core, tensor)

    def x_peer(by):
        return (((x + by) % RING) * CORES + core, tensor)

    def z_peer(by):
        return (dp, ((z + by) % RING) * RING + y)

    def y_peer(by):
        return (dp, z * RING + (y + by) % RING)

    def group_peer(i):
        return (dp, (tensor + i) % PARTS)

    chunk = w_buf.shape[2]

    def w_copy(i):
        return pltpu.make_async_copy(w_ref.at[:, pl.ds(i * chunk, chunk)], w_buf.at[i % 2], w_sem.at[i % 2])

    w_copy(0).start()
    w_copy(1).start()
    for s in range(steps):
        tiles[s, z, y] = hid_ref[s]

    barrier = pltpu.get_barrier_semaphore()
    for i in range(1, PARTS):
        pl.semaphore_signal(barrier, inc=1, device_id=group_peer(i), device_id_type=MESH)
    pl.semaphore_signal(barrier, inc=1, device_id=partner, device_id_type=MESH)
    for by in (1, RING - 1):
        pl.semaphore_signal(barrier, inc=1, device_id=x_peer(by), device_id_type=MESH)
    pl.semaphore_wait(barrier, PARTS + 2)

    def gather_ring(half, at, peer, base):
        right, left = (at + 1) % RING, (at + RING - 1) % RING

        def copy(n, r, h, by):
            ref = half(r, h)
            return remote(ref, ref, ag_send.at[base + n], ag_recv.at[base + n], peer(by))

        r1 = copy(0, at, 0, 1)
        l1 = copy(1, at, 1, RING - 1)
        r2 = copy(2, at, 1, 1)
        l2 = copy(3, at, 0, RING - 1)
        for c in (r1, l1, r2, l2):
            c.start()

        def pass_on():
            r1.wait()
            r3 = copy(4, left, 0, 1)
            r3.start()
            l1.wait()
            l3 = copy(5, right, 1, RING - 1)
            l3.start()

            def finish():
                for c in (r2, l2, r3, l3):
                    c.wait()

            return finish

        return pass_on

    def half_rows(s, at_z, at_y, h):
        return tiles.at[s, at_z, at_y, pl.ds(h * (sub // 2), sub // 2)]

    two = RING // 2
    p1 = gather_ring(lambda r, h: half_rows(0, z, r, h), y, y_peer, 0)
    q1 = gather_ring(lambda r, h: half_rows(1, r, y, h), z, z_peer, 6)

    def top_rows(at, size, best):
        part = arena[pl.ds(at, size), :].astype(F32)
        return jnp.maximum(best, jnp.max(part.reshape(size // 8, 8, tokens), axis=0))

    logits_in.wait()
    best = sweep(0, shard, 64, top_rows, jnp.full((8, tokens), LOW, F32))
    peak_here = jnp.max(best, axis=0, keepdims=True)

    def exp_rows(at, size, acc):
        part = jnp.exp(arena[pl.ds(at, size), :].astype(F32) - peak_here)
        for c in range(lane_parts):
            floats[c, pl.ds(at, size), :] = part[:, c * 128 : (c + 1) * 128]
        return acc + jnp.sum(part.reshape(size // 8, 8, tokens), axis=0)

    acc = sweep(0, shard, 64, exp_rows, jnp.zeros((8, tokens), F32))
    total_here = jnp.sum(acc, axis=0, keepdims=True)
    row8 = lax.broadcasted_iota(I32, (8, tokens), 0)
    ex1[tensor] = jnp.where(row8 == 0, peak_here, jnp.where(row8 == 1, total_here, 0.0))
    first = [
        remote(ex1.at[tensor], ex1.at[tensor], ex_send.at[0, i], ex_recv.at[0, i], group_peer(i))
        for i in range(1, PARTS)
    ]
    for copy in first:
        copy.start()

    ids = jnp.concatenate([ids_ref[...], jnp.full((PARTS, wide - block), -1, I32)], axis=1)
    local = ids - tensor * shard
    mine = (local >= 0) & (local < shard)
    own = jnp.sum(jnp.where(lax.broadcasted_iota(I32, (PARTS, wide), 0) == tensor, ids, 0), axis=0, keepdims=True)
    start = lax.broadcasted_iota(I32, (PARTS, wide), 0) * shard
    from_owner = (own >= start) & (own < start + shard)
    hits = jnp.concatenate([jnp.where(mine, 1.0, 0.0), jnp.where(from_owner, 1.0, 0.0)], axis=0)
    before = lax.broadcasted_iota(I32, (256, 256), 0)
    after = lax.broadcasted_iota(I32, (256, 256), 1)
    upper = jnp.where(before <= after, 1.0, 0.0).astype(BF16)
    seen = jnp.full((2 * PARTS, 1), -1.0, F32)
    rank_list = []
    for n in range(wide // 256):
        part = hits[:, n * 256 : (n + 1) * 256]
        rank_list.append(jnp.dot(part.astype(BF16), upper, preferred_element_type=F32) + seen)
        seen = seen + jnp.sum(part, axis=1, keepdims=True)
    ranks = jnp.concatenate(rank_list, axis=1)
    count_v[...] = jnp.broadcast_to(seen[:PARTS] + 1.0, count_v.shape)
    owner = lax.broadcasted_iota(I32, (PARTS, wide), 0).astype(F32) * float(slots)
    place = jnp.sum(jnp.where(from_owner, owner + ranks[PARTS:], 0.0), axis=0, keepdims=True)
    place_v[...] = jnp.clip(jnp.broadcast_to(place, (8, wide)).astype(I32), 0, PARTS * slots - 1)
    rank_v[0] = jnp.where(mine, ranks[:PARTS], -1.0)
    rank_v[1] = jnp.where(mine, local - (local & 255), 0).astype(F32)
    rank_v[2] = jnp.where(mine, local & 255, 0).astype(F32)
    to_place = pltpu.make_async_copy(place_v, place_s, s_sem.at[0])
    to_place.start()

    p1_end = p1()
    q1_end = q1()

    slot = (lax.broadcasted_iota(I32, (slots // 16, 16, wide), 0) * 16).astype(F32)
    slot = slot + lax.broadcasted_iota(I32, (slots // 16, 16, wide), 1).astype(F32)
    slot = (slot - 128.0).astype(BF16)
    kind = lax.broadcasted_iota(I32, (8, wide), 0)

    tab_v[...] = jnp.zeros_like(tab_v)

    def table_step(b, _):
        rank = jnp.minimum(rank_v[0, pl.ds(b, 1), :], float(slots)) - 128.0
        rank = jnp.broadcast_to(rank, (16, wide)).astype(BF16)
        info = jnp.where(kind == 0, rank_v[1, pl.ds(b, 1), :], jnp.where(kind == 1, rank_v[2, pl.ds(b, 1), :], 0.0))
        hot = jnp.where(slot == rank[None], jnp.ones((), BF16), jnp.zeros((), BF16)).reshape(slots, wide)
        got = lax.dot_general(info.astype(BF16), hot, NT, preferred_element_type=F32)
        found = (got[0:1, :] + got[1:2, :]).astype(I32)
        tab_v[pl.ds(b, 1), 0:slots] = jnp.clip(found, 0, shard - 1)
        return 0

    lax.fori_loop(0, two, table_step, 0)
    p1_end()
    q1_end()
    p2 = gather_ring(lambda r, h: tiles.at[0, r, pl.ds(h * two, two)], z, z_peer, 12)
    q2 = gather_ring(lambda r, h: tiles.at[1, pl.ds(h * two, two), r], y, y_peer, 18)
    lax.fori_loop(two, PARTS, table_step, 0)
    to_tab = pltpu.make_async_copy(tab_v, tab_s, s_sem.at[1])
    to_tab.start()

    for copy in first:
        copy.wait()
    peaks = [ex1[i, 0:1, :] for i in range(PARTS)]
    peak = functools.reduce(jnp.maximum, peaks)
    total = sum(ex1[i, 1:2, :] * jnp.exp(peaks[i] - peak) for i in range(PARTS))
    share = jnp.exp(peak_here - peak) / total
    to_tab.wait()
    to_place.wait()

    def pick(index_of, first, last):
        def go(i, _):
            got = []
            for r in range(16):
                at = index_of(i * 16 + r)
                got.append([floats[c, pl.ds(at, 1), :] for c in range(lane_parts)])
            for r in range(16):
                for c in range(lane_parts):
                    picked[c, pl.ds(i * 16 + r, 1), :] = got[r][c]
            return 0

        lax.fori_loop(first // 16, last // 16, go, 0)

    def joined(at, size):
        return jnp.concatenate([picked[c, pl.ds(at, size), :] for c in range(lane_parts)], axis=1)

    def out_at(i):
        return arena.at[pl.ds(pl.multiple_of(i * slots, 16), slots)]

    def in_at(i):
        return arena.at[pl.ds(pl.multiple_of((PARTS + i) * slots, 16), slots)]

    def sent(i):
        to = (tensor + i) % PARTS
        return remote(out_at(to), in_at(tensor), a2a_send.at[i], a2a_recv.at[i], (dp, to))

    row_of = lax.broadcasted_iota(I32, (slots, tokens), 0).astype(F32)

    def pick_into(to, ref, mass):
        pick(lambda j: tab_s[to, j], 0, slots)
        value = (joined(0, slots) * share).astype(BF16)
        ref[...] = value
        used = row_of < jnp.concatenate([count_v[pl.ds(to, 1), :]] * lane_parts, axis=1)
        value = jnp.where(used, value.astype(F32), 0.0)
        return mass + jnp.sum(value.reshape(slots // 8, 8, tokens), axis=0)

    def pick_step(i, mass):
        to = (tensor + i) % PARTS
        return pick_into(to, out_at(to), mass)

    def send_step(i, _):
        sent(i).start()
        return 0

    mass_here = lax.fori_loop(1, HELD, pick_step, jnp.zeros((8, tokens), F32))
    p2_end = p2()
    q2_end = q2()
    lax.fori_loop(1, HELD, send_step, 0)
    mass_here = lax.fori_loop(HELD, PARTS, pick_step, mass_here)
    mass_here = jnp.sum(pick_into(tensor, in_at(tensor), mass_here), axis=0, keepdims=True)

    p2_end()
    q2_end()
    lax.fori_loop(HELD, PARTS, send_step, 0)
    swap_h = [
        remote(
            tiles.at[s, :, pl.ds((1 - core) * CORES, CORES)],
            tiles.at[steps, :, pl.ds(s * CORES, CORES)],
            pair_send.at[4 + s],
            pair_recv.at[4 + s],
            partner,
        )
        for s in range(steps)
    ]
    for copy in swap_h:
        copy.start()

    pieces = PARTS * sub // chunk
    each = chunk // sub
    expo[...] = jnp.zeros((rows, both), F32)

    def score_step(i, _):
        w_copy(i).wait()
        for s in range(steps):
            at = i * each
            h = tiles[s, at // RING, pl.ds(at % RING, each)].reshape(chunk, tokens)
            lanes = slice(s * tokens, (s + 1) * tokens)
            expo[0:block, lanes] += jnp.dot(w_buf[i % 2], h, preferred_element_type=F32)

        @pl.when(i + 2 < pieces)
        def _():
            w_copy(i + 2).start()

        return 0

    lax.fori_loop(0, pieces, score_step, 0)

    per = RING * sub // chunk
    count = RING * per

    def w_row(i):
        order = (2, 1, RING - 1, 0)[i // per]
        return ((z + order) % RING) * per + i % per

    def w_again(i):
        at = pl.multiple_of(w_row(i) * chunk, chunk)
        return pltpu.make_async_copy(w_ref.at[:, pl.ds(at, chunk)], w_buf.at[i % 2], w_sem.at[i % 2])

    w_again(0).start()
    w_again(1).start()
    if rows > block:
        expo[block:rows, :] = jnp.full((rows - block, both), LOW, F32)

    def top_step(at, size, m):
        return jnp.maximum(m, jnp.max(expo[pl.ds(at, size), :].reshape(size // 8, 8, both), axis=0))

    top = sweep(0, rows, 32, top_step, jnp.full((8, both), LOW, F32))
    top = jnp.max(top, axis=0, keepdims=True)

    def exp_step(at, size, a):
        value = jnp.exp(expo[pl.ds(at, size), :] - top)
        expo[pl.ds(at, size), :] = value
        return a + jnp.sum(value.reshape(size // 8, 8, both), axis=0)

    weight = sweep(0, rows, 32, exp_step, jnp.zeros((8, both), F32))
    weight = jnp.sum(weight, axis=0, keepdims=True)

    own_rows = CORES * sub
    for i in range(RING):
        for s in range(steps):
            part = tiles[s, i, pl.ds(core * CORES, CORES)].reshape(own_rows, tokens)
            hn[i, s * tokens : (s + 1) * tokens, :] = part.T
    for copy in swap_h:
        copy.wait()
    for i in range(RING):
        for s in range(steps):
            part = tiles[steps, i, s * CORES : (s + 1) * CORES].reshape(own_rows, tokens)
            hn[i, both + s * tokens : both + (s + 1) * tokens, :] = part.T

    row8 = lax.broadcasted_iota(I32, (8, both), 0)
    mass_wide = jnp.concatenate([mass_here] * steps, axis=1)
    ex2[tensor] = jnp.where(row8 == 0, top, jnp.where(row8 == 1, weight, jnp.where(row8 == 2, mass_wide, 0.0)))
    second = [
        remote(ex2.at[tensor], ex2.at[tensor], ex_send.at[1, i], ex_recv.at[1, i], group_peer(i))
        for i in range(1, PARTS)
    ]
    for copy in second:
        copy.start()

    def widen_in(i):
        part = in_at(i)[...].astype(F32)
        for c in range(lane_parts):
            floats[c, pl.ds(pl.multiple_of(i * slots, 16), slots), :] = part[:, c * 128 : (c + 1) * 128]

    widen_in(tensor)

    def arrived(i, _):
        sent(i).wait()
        widen_in((tensor + PARTS - i) % PARTS)
        return 0

    lax.fori_loop(1, PARTS, arrived, 0)
    for copy in second:
        copy.wait()
    tops = [ex2[i, 0:1, :] for i in range(PARTS)]
    top_all = functools.reduce(jnp.maximum, tops)
    weight_all = sum(ex2[i, 1:2, :] * jnp.exp(tops[i] - top_all) for i in range(PARTS))
    mass = sum(ex2[i, 2:3, 0:tokens] for i in range(PARTS))

    scales = [LOSS_SCALE * STEP_DECAY**s for s in range(steps)]

    def shift(value, step):
        if step == 0:
            return value
        lane = lax.broadcasted_iota(I32, value.shape, 1)
        return jnp.where(lane < tokens - step, pltpu.roll(value, tokens - step, 1), 0.0)

    factor = jnp.exp(top - top_all) / weight_all
    coefs = []
    for s in range(steps):
        mass_of = shift(jnp.broadcast_to(mass, (8, tokens)), s)[0:1, :]
        coefs.append(scales[s] * mass_of * factor[:, s * tokens : (s + 1) * tokens])

    def slope_step(at, size, _):
        prob = joined(at, size)
        for s in range(steps):
            lanes = slice(s * tokens, (s + 1) * tokens)
            value = expo[pl.ds(at, size), lanes] * coefs[s] - scales[s] * shift(prob, s)
            sl[pl.ds(at, size), lanes] = value.astype(BF16)
        return 0

    def link(n, src, dst, device):
        return remote(src, dst, ring_send.at[n], ring_recv.at[n], device)

    cuts = pieces_of(rows)
    half = rows // 2

    def head_part(by, at, size):
        return jnp.dot(sl[at : at + size, :], hn[(x + by) % RING], preferred_element_type=F32)

    def x_piece(slot, by, cut, into, to, n, far=None):
        at, size = cuts[cut]
        value = head_part(by, at, size)
        spot = pl.ds(at - cut // 2 * half, size)
        if far is not None:
            value = value + x_far[far, spot, :].astype(F32)
        x_out[slot, spot, :] = value.astype(BF16)
        copy = link(n, x_out.at[slot, spot], into.at[spot], x_peer(to))
        copy.start()
        return copy

    def x_send(slot, by, h, into, to, base, far=None):
        return [x_piece(slot, by, 2 * h + n, into, to, base + n, far) for n in range(2)]

    far_of = [None] * 4
    waiting = []

    def send_far():
        cut, copy = waiting.pop()
        copy.wait()
        h = cut // 2
        far_of[cut] = x_piece(h, 2, cut, x_far.at[h], (1, RING - 1)[h], cut)

    for cut in (0, 2, 1, 3):
        at, size = cuts[cut]
        pick(lambda j: place_s[0, j], at, at + size)
        if at + size > block:
            for c in range(lane_parts):
                picked[c, block : at + size, :] = jnp.zeros((at + size - block, 128), F32)
        sweep(at, at + size, 96, slope_step, 0)
        swap = remote(
            sl.at[pl.ds(at, size), pl.ds(0, both)],
            sl.at[pl.ds(at, size), pl.ds(both, both)],
            pair_send.at[cut],
            pair_recv.at[cut],
            partner,
        )
        swap.start()
        if waiting:
            send_far()
        waiting.append((cut, swap))
    send_far()
    far_r, far_l = far_of[:2], far_of[2:]
    free_r = x_send(2, 1, 1, x_in.at[1], 1, 4)
    free_l = x_send(3, RING - 1, 0, x_in.at[2], RING - 1, 6)

    for at in range(0, rows, 128):
        size = min(128, rows - at)
        flat[:, at : at + size] = sl[at : at + size, 0:both].T

    def term_step(i):
        w_again(i).wait()
        value = jnp.dot(flat[:, 0:block], w_buf[i % 2], preferred_element_type=F32)
        first = w_row(i) * chunk
        flipped = value.T
        for lane in range(both // 128):
            spot = pl.ds(pl.multiple_of(lane % lane_parts * PARTS * sub + first, chunk), chunk)
            floats[lane // lane_parts, spot, :] = flipped[:, lane * 128 : (lane + 1) * 128]
        if i + 2 < count:
            w_again(i + 2).start()

    pair_of = RING // 2

    def spot_of(n, c, first, size):
        return pl.ds(pl.multiple_of((c * PARTS + n) * sub + first, 32), size)

    def term(s, n, first=0, size=sub):
        return jnp.concatenate([floats[s, spot_of(n, c, first, size), :] for c in range(lane_parts)], axis=1)

    def term_add(s, n, more):
        for c in range(lane_parts):
            spot = spot_of(n, c, 0, sub)
            floats[s, spot, :] = floats[s, spot, :] + more[:, c * 128 : (c + 1) * 128]

    def p_term(by, n):
        return term(0, ((z + by) % RING) * RING + n)

    def q_term(by, n):
        return term(1, n * RING + (y + by) % RING)

    class Blocks:
        def __init__(self, first, halves):
            self.first, self.halves = first, halves

        def ref(self, slot, n=None):
            if self.halves:
                at = self.first + slot // 2
                return tiles.at[at // PARTS, at // RING % RING, at % RING, pl.ds(slot % 2 * (sub // 2), sub // 2)]
            at = self.first + 2 * slot
            group = tiles.at[at // PARTS, at // RING % RING]
            return group.at[pl.ds(at % RING, 2)] if n is None else group.at[at % RING + n]

        def __getitem__(self, key):
            return self.ref(*key)[...]

    p_out, p_far, p_in = Blocks(0, False), Blocks(12, False), Blocks(16, False)
    q_out, q_far, q_in = Blocks(24, False), Blocks(36, False), Blocks(40, False)
    p2_out, p2_far, p2_in = Blocks(48, True), Blocks(51, True), Blocks(52, True)
    q2_out, q2_far, q2_in = Blocks(54, True), Blocks(57, True), Blocks(58, True)

    def ring_sum(part, out, far, into, peer, base):
        def put(slot, by, h, extra=None):
            for n, value in enumerate(part(by, h)):
                if extra is not None:
                    value = value + far[extra, n].astype(F32)
                out.ref(slot, n)[...] = value.astype(BF16)

        def start(n, slot, dst, by):
            copy = link(base + n, out.ref(slot), dst, peer(by))
            copy.start()
            return copy

        held = {}

        def begin():
            put(0, 2, 0)
            held["a"] = start(0, 0, far.ref(0), 1)
            put(1, 2, 1)
            held["b"] = start(1, 1, far.ref(1), RING - 1)

        def free():
            put(3, 1, 1)
            held["c"] = start(2, 3, into.ref(1), 1)
            put(4, RING - 1, 0)
            held["d"] = start(3, 4, into.ref(2), RING - 1)

        def late():
            held["a"].wait()
            put(2, 1, 0, 0)
            held["e"] = start(4, 2, into.ref(0), 1)
            held["b"].wait()
            put(5, RING - 1, 1, 1)
            held["f"] = start(5, 5, into.ref(3), RING - 1)

        def end():
            for name in "cdef":
                held[name].wait()

        return begin, free, late, end

    def p_part(by, h):
        return [p_term(by, h * pair_of + n) for n in range(pair_of)]

    def q_part(by, h):
        return [q_term(by, h * pair_of + n) for n in range(pair_of)]

    p_begin, p_free, p_late, p_end = ring_sum(p_part, p_out, p_far, p_in, z_peer, 12)
    q_begin, q_free, q_late, q_end = ring_sum(q_part, q_out, q_far, q_in, y_peer, 18)
    for i in range(count):
        term_step(i)
        if i + 1 == per:
            p_begin()
        if i + 1 == 3 * per:
            p_free()
    q_begin()
    q_free()
    p_late()
    q_late()

    for copy in far_r:
        copy.wait()
    dep_r = x_send(0, 1, 0, x_in.at[0], 1, 8, far=0)
    for copy in far_l:
        copy.wait()
    dep_l = x_send(1, RING - 1, 1, x_in.at[3], RING - 1, 10, far=1)

    for at, size in cuts:
        keep = min(size, block - at)
        gw_ref[at : at + keep, :] = head_part(0, at, size)[0:keep]

    p_end()
    for n in range(RING):
        got = p_in[n // pair_of, n % pair_of].astype(F32) + p_in[2 + n // pair_of, n % pair_of].astype(F32)
        term_add(0, z * RING + n, got)
    q_end()
    for n in range(RING):
        got = q_in[n // pair_of, n % pair_of].astype(F32) + q_in[2 + n // pair_of, n % pair_of].astype(F32)
        term_add(1, n * RING + y, got)

    cut = sub // 2

    def p2_part(by, h):
        return [term(0, z * RING + (y + by) % RING, h * cut, cut)]

    def q2_part(by, h):
        return [term(1, ((z + by) % RING) * RING + y, h * cut, cut)]

    p2 = ring_sum(p2_part, p2_out, p2_far, p2_in, y_peer, 24)
    q2 = ring_sum(q2_part, q2_out, q2_far, q2_in, z_peer, 30)
    for stage in range(4):
        p2[stage]()
        q2[stage]()
    for s, into in enumerate((p2_in, q2_in)):
        for h in range(2):
            value = term(s, tensor, h * cut, cut)
            value = value + into[h, 0].astype(F32) + into[2 + h, 0].astype(F32)
            gh_ref[s, h * cut : (h + 1) * cut, :] = value.astype(BF16)

    def add_in(at, size, h):
        to = at + h * half
        got = x_in[h, pl.ds(at, size), :].astype(F32) + x_in[2 + h, pl.ds(at, size), :].astype(F32)
        keep = min(size, block - to)
        gw_ref[to : to + keep, :] = gw_ref[to : to + keep, :] + got[0:keep]

    for h, from_left, from_right in ((0, dep_r, free_l), (1, free_r, dep_l)):
        for n in range(2):
            from_left[n].wait()
            from_right[n].wait()
            at, size = cuts[2 * h + n]
            for i in range(0, size, 16):
                add_in(at - h * half + i, 16, h)


def both_gradients(hid, ids, logits, w, slots):
    steps, sub, tokens = hid.shape
    parts, block = ids.shape
    shard = logits.shape[0]
    both = steps * tokens
    rows = ceil_to(block, 32)
    wide = ceil_to(block, 256)
    width = CORES * sub
    lane_parts = tokens // 128
    half = rows // 2
    depth = max(ceil_to(max(shard, parts * slots), 32), lane_parts * parts * sub)
    vmem = pl.BlockSpec(memory_space=pltpu.VMEM)
    hbm = pl.BlockSpec(memory_space=pl.ANY)
    dma = pltpu.SemaphoreType.DMA
    return pl.pallas_call(
        functools.partial(kernel, (steps, tokens, block, rows, slots)),
        out_shape=(
            jax.ShapeDtypeStruct((steps, sub, tokens), BF16),
            jax.ShapeDtypeStruct((block, width), F32),
        ),
        in_specs=[vmem, vmem, hbm, hbm],
        out_specs=(vmem, vmem),
        scratch_shapes=[
            pltpu.VMEM((2 + steps, RING, RING, sub, tokens), BF16),
            pltpu.VMEM((shard, tokens), BF16),
            pltpu.VMEM((lane_parts, depth, 128), F32),
            pltpu.VMEM((RING, CORES * both, width), BF16),
            pltpu.VMEM((rows, CORES * both), BF16),
            pltpu.VMEM((2, block, 2 * sub), BF16),
            pltpu.VMEM((lane_parts, rows, 128), F32),
            pltpu.VMEM((rows, both), F32),
            pltpu.VMEM((both, ceil_to(rows, 128)), BF16),
            pltpu.VMEM((3, parts, wide), F32),
            pltpu.VMEM((parts, 128), F32),
            pltpu.VMEM((parts, ceil_to(slots, 128)), I32),
            pltpu.VMEM((8, wide), I32),
            pltpu.VMEM((parts, 8, tokens), F32),
            pltpu.VMEM((parts, 8, both), F32),
            pltpu.VMEM((4, half, width), BF16),
            pltpu.VMEM((2, half, width), BF16),
            pltpu.VMEM((4, half, width), BF16),
            pltpu.SMEM((parts, ceil_to(slots, 128)), I32),
            pltpu.SMEM((8, wide), I32),
            dma((24,)),
            dma((24,)),
            dma((parts,)),
            dma((parts,)),
            dma((2, parts)),
            dma((2, parts)),
            dma((6,)),
            dma((6,)),
            dma((2,)),
            dma((3,)),
            dma((36,)),
            dma((36,)),
        ],
        compiler_params=pltpu.CompilerParams(
            collective_id=2, has_side_effects=True, vmem_limit_bytes=63 * 2**20
        ),
        name="both_gradients",
    )(hid, ids, logits, w)


def hand_on_kernel(gh_in, gw_in, gh_out, gw_out, gh_held, gw_held, in_sem, out_sem):
    block = gw_in.shape[0]
    size = ceil_to(-(-block // 8), 8)
    pairs = [(gh_in, gh_held, gh_out)]
    for at in range(0, block, size):
        rows = pl.ds(at, min(size, block - at))
        pairs.append((gw_in.at[rows], gw_held.at[rows], gw_out.at[rows]))
    loads = [pltpu.make_async_copy(src, held, in_sem.at[n]) for n, (src, held, _) in enumerate(pairs)]
    stores = [pltpu.make_async_copy(held, dst, out_sem.at[n]) for n, (_, held, dst) in enumerate(pairs)]
    for copy in loads:
        copy.start()
    for load, store in zip(loads, stores):
        load.wait()
        store.start()
    for store in stores:
        store.wait()


def hand_on(gh, gw):
    hbm = pl.BlockSpec(memory_space=pl.ANY)
    return pl.pallas_call(
        hand_on_kernel,
        out_shape=(jax.ShapeDtypeStruct(gh.shape, gh.dtype), jax.ShapeDtypeStruct(gw.shape, gw.dtype)),
        in_specs=[hbm, hbm],
        out_specs=(hbm, hbm),
        scratch_shapes=[
            pltpu.VMEM(gh.shape, gh.dtype),
            pltpu.VMEM(gw.shape, gw.dtype),
            pltpu.SemaphoreType.DMA((9,)),
            pltpu.SemaphoreType.DMA((9,)),
        ],
        compiler_params=pltpu.CompilerParams(vmem_limit_bytes=50 * 2**20),
        name="hand_on",
    )(gh, gw)


def per_device(hidden, draft_head, target_logits, draft_to_target):
    steps, tokens, _ = hidden.shape
    block = draft_to_target.shape[0] // PARTS
    heavy = block // 8
    bound = heavy + (block - heavy + PARTS - 1) // PARTS
    slots = ceil_to(bound, 16)
    w = draft_head.T
    ids = draft_to_target.reshape(PARTS, block)
    gh, gw = hand_on(*both_gradients(hidden.transpose(0, 2, 1), ids, target_logits.T, w, slots))
    return gh.transpose(0, 2, 1), gw.T


def solution(mesh):
    in_specs = (P(None, "dp", "tensor"), P(None, "tensor"), P("dp", "tensor"), P())
    out_specs = (P(None, "dp", "tensor"), P("dp", "tensor"))
    return jax.shard_map(
        per_device, mesh=mesh, in_specs=in_specs, out_specs=out_specs, check_vma=False
    )
```
